32 devices in a mesh: af: 8 (over z, core), ha: 4 (over y, x).
Axes of the slice: x: 2, y: 2, z: 4, core: 2. Of those that a mesh axis runs over, the one named last changes fastest.
Arguments:
- block_input: bfloat16 [4096, 1024], P(('af', 'ha')), may hold values from -6 to 6
- lengths: int32 [8, 3], P('af'), may hold values from 16 to 480, as said below
- cotangent: bfloat16 [4096, 1024], P(('af', 'ha')), may hold values from -6 to 6
- attngain_early: float32 [1024], replicated, may hold values from 0.25 to 1.75
- query_early: bfloat16 [1024, 1024], P('af', 'ha'), may hold values from -0.1875 to 0.1875
- keys_early: bfloat16 [1024, 1024], P('af', 'ha'), may hold values from -0.1875 to 0.1875
- values_early: bfloat16 [1024, 1024], P('af', 'ha'), may hold values from -0.1875 to 0.1875
- output_early: bfloat16 [1024, 1024], P('af', 'ha'), may hold values from -1.5 to 1.5
- ffngain_early: float32 [1024], replicated, may hold values from 0.25 to 1.75
- gate_early: bfloat16 [1024, 2816], P('af', 'ha'), may hold values from -0.1875 to 0.1875
- upward_early: bfloat16 [1024, 2816], P('af', 'ha'), may hold values from -0.1875 to 0.1875
- down_early: bfloat16 [1024, 2816], P('af', 'ha'), may hold values from -0.109375 to 0.109375
- attngain_later: float32 [1024], replicated, may hold values from 0.25 to 1.75
- query_later: bfloat16 [1024, 1024], P('af', 'ha'), may hold values from -0.1875 to 0.1875
- keys_later: bfloat16 [1024, 1024], P('af', 'ha'), may hold values from -0.1875 to 0.1875
- values_later: bfloat16 [1024, 1024], P('af', 'ha'), may hold values from -0.1875 to 0.1875
- output_later: bfloat16 [1024, 1024], P('af', 'ha'), may hold values from -1.5 to 1.5
- ffngain_later: float32 [1024], replicated, may hold values from 0.25 to 1.75
- gate_later: bfloat16 [1024, 2816], P('af', 'ha'), may hold values from -0.1875 to 0.1875
- upward_later: bfloat16 [1024, 2816], P('af', 'ha'), may hold values from -0.1875 to 0.1875
- down_later: bfloat16 [1024, 2816], P('af', 'ha'), may hold values from -0.109375 to 0.109375
Outputs:
- block_output: bfloat16 [4096, 1024], P(('af', 'ha'))
- input_grad: float32 [4096, 1024], P(('af', 'ha'))
- attngaingrad_early: float32 [1024], replicated
- querygrad_early: float32 [1024, 1024], P('af', 'ha')
- keysgrad_early: float32 [1024, 1024], P('af', 'ha')
- valuesgrad_early: float32 [1024, 1024], P('af', 'ha')
- outputgrad_early: float32 [1024, 1024], P('af', 'ha')
- ffngaingrad_early: float32 [1024], replicated
- gategrad_early: float32 [1024, 2816], P('af', 'ha')
- upwardgrad_early: float32 [1024, 2816], P('af', 'ha')
- downgrad_early: float32 [1024, 2816], P('af', 'ha')
- attngaingrad_later: float32 [1024], replicated
- querygrad_later: float32 [1024, 1024], P('af', 'ha')
- keysgrad_later: float32 [1024, 1024], P('af', 'ha')
- valuesgrad_later: float32 [1024, 1024], P('af', 'ha')
- outputgrad_later: float32 [1024, 1024], P('af', 'ha')
- ffngaingrad_later: float32 [1024], replicated
- gategrad_later: float32 [1024, 2816], P('af', 'ha')
- upwardgrad_later: float32 [1024, 2816], P('af', 'ha')
- downgrad_later: float32 [1024, 2816], P('af', 'ha')
The draws below stay inside these ranges and needn't reach their ends.
Inputs may be any that keep to these rules, and one draw needn't show every extreme that they name: Row b lists the lengths of the 3 sequences of bucket b in their order; padding fills the rest of its 512 tokens and is at most 32 tokens. One sequence of every bucket begins within the bucket's first 128 tokens and ends within its last 128.
All inputs are finite; a program needn't handle non-finite values.
Results may differ from the reference program's by a relative error of at most 0.035.
Values may be sent and summed in bfloat16 or wider, within the bound.
A program may use at most 128 MiB of HBM per device.

```python
import jax
import jax.numpy as jnp
from jax import lax

D = 1024
HEADS = 16
HD = 64
FF = 2816
TOK_DEV = 128
SEQS = 3
BUCKET = 512
BUCKETS = 8
TOKENS = 4096


def draw_lengths(key, part):
    key = jax.random.fold_in(key, 11)
    splits = jax.random.split(key, 4)
    shortest = TOK_DEV // 8
    short_most = TOK_DEV // 4
    shorts = jax.random.randint(splits[0], (BUCKETS, SEQS - 1), shortest, short_most + 1, dtype=jnp.int32)
    padding = jax.random.randint(splits[1], (BUCKETS,), 0, TOK_DEV // 4 + 1, dtype=jnp.int32)
    chosen = jax.random.randint(splits[2], (), 0, BUCKETS, dtype=jnp.int32)
    picked = jnp.arange(BUCKETS, dtype=jnp.int32) == chosen
    shorts = jnp.where(picked[:, None], shortest, shorts)
    padding = jnp.where(picked, 0, padding)
    longest = BUCKET - padding - jnp.sum(shorts, axis=1).astype(jnp.int32)
    placed = jax.random.randint(splits[3], (BUCKETS, 1), 0, SEQS, dtype=jnp.int32)
    columns = jnp.arange(SEQS, dtype=jnp.int32)
    earlier_cols = jnp.take(shorts, jnp.clip(columns, 0, SEQS - 2), axis=1)
    later_cols = jnp.take(shorts, jnp.clip(columns - 1, 0, SEQS - 2), axis=1)
    result = jnp.where(columns[None, :] < placed, earlier_cols, jnp.where(columns[None, :] == placed, longest[:, None], later_cols))
    return result.astype(jnp.int32)


def block_scale(rng, extent, cuts, smallest, top_value):
    factor_of, own = 1.0, jax.random.fold_in(rng, 6)
    for dim, shards_of in cuts:
        draws = jnp.exp(jax.random.uniform(jax.random.fold_in(own, dim), (shards_of,), jnp.float32, smallest / len(cuts), top_value / len(cuts)))
        factor_of = factor_of * jnp.repeat(draws, extent[dim] // shards_of).reshape([-1 if axis == dim else 1 for axis in range(len(extent))])
    return factor_of


def normal_values(own_key, shape, deviation, limit, cuts=(), kind=jnp.bfloat16):
    drawn = jax.random.normal(own_key, shape, jnp.float32) * deviation
    if len(cuts) > 0:
        drawn = block_scale(own_key, shape, cuts, -0.22, 0.18) * drawn
    return jnp.clip(drawn, min=-limit, max=limit).astype(kind)


def setup_inputs(seed: int = 0) -> dict:
    arg_keys = jax.random.split(jax.random.key(seed), 22)
    block_input = normal_values(arg_keys[0], (TOKENS, D), 1.0, 6.0, ((0, 32),))
    lengths = draw_lengths(jax.random.fold_in(arg_keys[21], 71), 0)
    cotangent = normal_values(arg_keys[2], (TOKENS, D), 1.0, 6.0, ((0, 32),))
    attngain_early = jnp.clip(1.0 + 0.15 * jax.random.normal(arg_keys[3], (D,), jnp.float32), 0.25, 1.75)
    query_early = normal_values(arg_keys[4], (D, D), D ** -0.5, 0.1875, ((0, 8), (1, 4)))
    keys_early = normal_values(arg_keys[5], (D, D), D ** -0.5, 0.1875, ((0, 8), (1, 4)))
    values_early = normal_values(arg_keys[6], (D, D), D ** -0.5, 0.1875, ((0, 8), (1, 4)))
    output_early = normal_values(arg_keys[7], (D, D), (D // 64) ** -0.5, 1.5, ((0, 8), (1, 4)))
    ffngain_early = jnp.clip(1.0 + 0.15 * jax.random.normal(arg_keys[8], (D,), jnp.float32), 0.25, 1.75)
    gate_early = normal_values(arg_keys[9], (D, FF), D ** -0.5, 0.1875, ((0, 8), (1, 4)))
    upward_early = normal_values(arg_keys[10], (D, FF), D ** -0.5, 0.1875, ((0, 8), (1, 4)))
    down_early = normal_values(arg_keys[11], (D, FF), FF ** -0.5, 0.109375, ((0, 8), (1, 4)))
    attngain_later = jnp.clip(1.0 + 0.15 * jax.random.normal(arg_keys[12], (D,), jnp.float32), 0.25, 1.75)
    query_later = normal_values(arg_keys[13], (D, D), D ** -0.5, 0.1875, ((0, 8), (1, 4)))
    keys_later = normal_values(arg_keys[14], (D, D), D ** -0.5, 0.1875, ((0, 8), (1, 4)))
    values_later = normal_values(arg_keys[15], (D, D), D ** -0.5, 0.1875, ((0, 8), (1, 4)))
    output_later = normal_values(arg_keys[16], (D, D), (D // 64) ** -0.5, 1.5, ((0, 8), (1, 4)))
    ffngain_later = jnp.clip(1.0 + 0.15 * jax.random.normal(arg_keys[17], (D,), jnp.float32), 0.25, 1.75)
    gate_later = normal_values(arg_keys[18], (D, FF), D ** -0.5, 0.1875, ((0, 8), (1, 4)))
    upward_later = normal_values(arg_keys[19], (D, FF), D ** -0.5, 0.1875, ((0, 8), (1, 4)))
    down_later = normal_values(arg_keys[20], (D, FF), FF ** -0.5, 0.109375, ((0, 8), (1, 4)))
    return {"block_input": block_input, "lengths": lengths, "cotangent": cotangent, "attngain_early": attngain_early, "query_early": query_early, "keys_early": keys_early, "values_early": values_early, "output_early": output_early, "ffngain_early": ffngain_early, "gate_early": gate_early, "upward_early": upward_early, "down_early": down_early, "attngain_later": attngain_later, "query_later": query_later, "keys_later": keys_later, "values_later": values_later, "output_later": output_later, "ffngain_later": ffngain_later, "gate_later": gate_later, "upward_later": upward_later, "down_later": down_later}


@jax.custom_vjp
def low(v):
    return lax.optimization_barrier(v.astype(jnp.bfloat16)).astype(jnp.float32)

@jax.custom_vjp
def low_back(v):
    return v

def low_keep(v):
    return (low(v), None)

def low_pass(kept, grad):
    return (grad,)

def back_keep(v):
    return (v, None)

def back_low(kept, grad):
    return (low(grad),)
low.defvjp(low_keep, low_pass)
low_back.defvjp(back_keep, back_low)
epsilon = 1e-06
rope_base = 10000.0

def matmul(left, right):
    return jnp.dot(left, right, precision=lax.Precision.HIGHEST)

def normalize(values, gain):
    return values * lax.rsqrt(lax.optimization_barrier(jnp.mean(values * values, axis=-1, keepdims=True)) + epsilon) * gain

def layout(lens_row):
    counted = lens_row.shape[0]
    ends = jnp.cumsum(lens_row).astype(jnp.int32)
    starts = (ends - lens_row).astype(jnp.int32)
    places = jnp.arange(BUCKET, dtype=jnp.int32)
    documents = lax.optimization_barrier(jnp.sum((places[:, None] >= ends[None, :]).astype(jnp.int32), axis=1)).astype(jnp.int32)
    validity = documents < counted
    matching = documents[:, None] == jnp.arange(counted, dtype=jnp.int32)[None, :]
    beginning = lax.optimization_barrier(jnp.sum(jnp.where(matching, starts[None, :], 0), axis=1)).astype(jnp.int32)
    offsets = (places - beginning).astype(jnp.float32)
    halfway = HD // 2
    frequency = rope_base ** (-jnp.arange(halfway, dtype=jnp.float32) / halfway)
    angles = offsets[:, None] * frequency[None, :]
    return (documents, places, validity, jnp.cos(angles)[:, None, :], jnp.sin(angles)[:, None, :])

def rotate(values, cos_table, sin_table):
    halfway = values.shape[-1] // 2
    former = values[..., :halfway]
    latter = values[..., halfway:]
    return jnp.concatenate([former * cos_table - latter * sin_table, latter * cos_table + former * sin_table], axis=-1)

def allowed_pairs(query_docs, query_places, query_valid, documents, places):
    causal = (query_docs[:, None] == documents[None, :]) & (places[None, :] <= query_places[:, None]) & query_valid[:, None]
    return causal | (places[None, :] == query_places[:, None])

def attention(queries, keys_rot, values_low, geometry):
    documents, places, validity = (geometry[0], geometry[1], geometry[2])
    block_rows = min(512, BUCKET)
    block_count = BUCKET // block_rows
    scaling = HD ** (-0.5)

    def attend_block(item):
        query_block, query_docs, query_places, query_valid = item
        allowed = allowed_pairs(query_docs, query_places, query_valid, documents, places)
        scores = low_back(jnp.einsum('qhd,khd->hqk', query_block, keys_rot, precision=lax.Precision.HIGHEST)) * scaling
        masked = jnp.where(allowed[None], scores, -1000000000.0)
        maximum = lax.optimization_barrier(jnp.max(masked, axis=-1, keepdims=True))
        weights = jnp.exp(masked - maximum)
        probs = low(weights / lax.optimization_barrier(jnp.sum(weights, axis=-1, keepdims=True)))
        return jnp.einsum('hqk,khd->qhd', probs, values_low, precision=lax.Precision.HIGHEST)
    items = (queries.reshape(block_count, block_rows, HEADS, HD), documents.reshape(block_count, block_rows), places.reshape(block_count, block_rows), validity.reshape(block_count, block_rows))
    result = lax.map(jax.checkpoint(attend_block), items)
    return result.reshape(BUCKET, HEADS * HD)

def layer_forward(rows, params, geometry, first_values):
    attngain, query, keys, values, output, ffngain, gate, upward, downward = params
    normed = low(normalize(rows, attngain))
    query_raw = low_back(matmul(normed, query))
    keys_raw = low_back(matmul(normed, keys))
    values_raw = low_back(matmul(normed, values))
    mixed = values_raw if first_values is None else 0.5 * values_raw + 0.5 * first_values
    queries = low(rotate(query_raw.reshape(BUCKET, HEADS, HD), geometry[3], geometry[4]))
    keys_rot = low(rotate(keys_raw.reshape(BUCKET, HEADS, HD), geometry[3], geometry[4]))
    values_low = low(mixed.reshape(BUCKET, HEADS, HD))
    attended = low(low_back(attention(queries, keys_rot, values_low, geometry)))
    middle = rows + low_back(matmul(attended, output.T))
    normed_mid = low(normalize(middle, ffngain))
    gate_raw = low_back(matmul(normed_mid, gate))
    upward_raw = low_back(matmul(normed_mid, upward))
    hidden = low(jax.nn.silu(gate_raw) * upward_raw)
    return (middle + low_back(matmul(hidden, downward.T)), values_raw)

def reference(block_input, lengths, cotangent, attngain_early, query_early, keys_early, values_early, output_early, ffngain_early, gate_early, upward_early, down_early, attngain_later, query_later, keys_later, values_later, output_later, ffngain_later, gate_later, upward_later, down_later):
    weights = (attngain_early, query_early, keys_early, values_early, output_early, ffngain_early, gate_early, upward_early, down_early, attngain_later, query_later, keys_later, values_later, output_later, ffngain_later, gate_later, upward_later, down_later)
    params = tuple((weight.astype(jnp.float32) for weight in weights))
    inputs = block_input.astype(jnp.float32).reshape(BUCKETS, BUCKET, D)
    seeds = cotangent.astype(jnp.float32).reshape(BUCKETS, BUCKET, D)

    def bucket_step(totals, item):
        rows, lens_row, seed_grad = item
        geometry = layout(lens_row)

        def forward(rows_in, params_in):
            middle_out, first_values = layer_forward(rows_in, params_in[:9], geometry, None)
            final_out, unused_values = layer_forward(middle_out, params_in[9:], geometry, first_values)
            return final_out
        final_out, pullback = jax.vjp(forward, rows, params)
        grad_rows, grad_params = pullback(seed_grad)
        totals = tuple((total + grad for total, grad in zip(totals, grad_params)))
        return (totals, (final_out, grad_rows))
    zeros = tuple((jnp.zeros(param.shape, jnp.float32) for param in params))
    totals, (outputs, grad_rows) = lax.scan(bucket_step, zeros, (inputs, lengths, seeds))
    return (outputs.reshape(TOKENS, D).astype(jnp.bfloat16), grad_rows.reshape(TOKENS, D), totals[0], totals[1], totals[2], totals[3], totals[4], totals[5], totals[6], totals[7], totals[8], totals[9], totals[10], totals[11], totals[12], totals[13], totals[14], totals[15], totals[16], totals[17])
```

```python
import functools

import jax
import jax.numpy as jnp
from jax import lax
from jax.experimental import pallas as pl
from jax.experimental.pallas import tpu as pltpu
from jax.sharding import PartitionSpec as P

HD = 64
epsilon = 1e-06
rope_base = 10000.0
MESH = pl.DeviceIdType.MESH
VMEM = pl.BlockSpec(memory_space=pltpu.VMEM)
ANY = pl.BlockSpec(memory_space=pl.ANY)
F32 = jnp.float32
BF16 = jnp.bfloat16


def mm(left, right):
    return jnp.dot(left, right, preferred_element_type=F32)


def mm_nt(left, right):
    return lax.dot_general(left, right, (((1,), (1,)), ((), ())), preferred_element_type=F32)


def mm_tn(left, right):
    return lax.dot_general(left, right, (((0,), (0,)), ((), ())), preferred_element_type=F32)


def normalize(values, gain):
    return values * lax.rsqrt(jnp.mean(values * values, axis=-1, keepdims=True) + epsilon) * gain


def norm_back(values, gain, grads):
    scaling = lax.rsqrt(jnp.mean(values * values, axis=-1, keepdims=True) + epsilon)
    weighted = gain * grads
    inner = jnp.mean(weighted * values, axis=-1, keepdims=True)
    return (
        scaling * weighted - values * scaling * scaling * scaling * inner,
        jnp.sum(grads * values * scaling, axis=0, keepdims=True),
    )


def layout(lens_row, bucket, head_count):
    counted = lens_row.shape[0]
    ends = jnp.cumsum(lens_row)
    starts = ends - lens_row
    places = jnp.arange(bucket, dtype=jnp.int32)
    documents = jnp.sum((places[:, None] >= ends[None, :]).astype(jnp.int32), axis=1)
    matching = documents[:, None] == jnp.arange(counted, dtype=jnp.int32)[None, :]
    beginning = jnp.sum(jnp.where(matching, starts[None, :], 0), axis=1)
    offsets = (places - beginning).astype(F32)
    halfway = HD // 2
    frequency = rope_base ** (-jnp.arange(halfway, dtype=F32) / halfway)
    angles = offsets[:, None] * frequency[None, :]
    cosine, sine = jnp.cos(angles), jnp.sin(angles)
    cos_table = jnp.tile(jnp.concatenate([cosine, cosine], axis=1), (1, head_count))
    sin_table = jnp.tile(jnp.concatenate([-sine, sine], axis=1), (1, head_count))
    query_docs = jnp.where(documents < counted, documents, -1)[:, None]
    return (cos_table, sin_table, query_docs, documents[None, :])


def other(me, k):
    result, bit = me, 1
    while bit <= k:
        if k & bit:
            result = result + bit * (1 - 2 * lax.rem(lax.div(me, bit), 2))
        bit *= 2
    return result


def greet(n, me):
    barrier = pltpu.get_barrier_semaphore()
    for k in range(1, n):
        pl.semaphore_signal(barrier, inc=1, device_id={"ha": other(me, k)}, device_id_type=MESH)


def met(n):
    pl.semaphore_wait(pltpu.get_barrier_semaphore(), n - 1)


def rows_of(index, count):
    return pl.ds(pl.multiple_of(index * count, count), count)


def gather_copy(buffer, me, target, rows, send, recv, slot):
    mine = buffer.at[rows_of(me, rows)]
    return pltpu.make_async_remote_copy(
        src_ref=mine, dst_ref=mine, send_sem=send.at[slot], recv_sem=recv.at[slot],
        device_id={"ha": target}, device_id_type=MESH,
    )


def start_gather(buffer, n, me, rows, send, recv):
    for k in range(1, n):
        gather_copy(buffer, me, other(me, k), rows, send, recv, k).start()


def wait_block(buffer, me, k, rows, send, recv):
    theirs = buffer.at[rows_of(other(me, k), rows)]
    pltpu.make_async_remote_copy(
        src_ref=theirs, dst_ref=theirs, send_sem=send.at[k], recv_sem=recv.at[k],
        device_id={"ha": other(me, k)}, device_id_type=MESH,
    ).wait_recv()


def wait_sent(buffer, n, me, rows, send, recv):
    for k in range(1, n):
        gather_copy(buffer, me, other(me, k), rows, send, recv, k).wait_send()


def part_copy(sbuf, rbuf, k, target, send, recv):
    return pltpu.make_async_remote_copy(
        src_ref=sbuf.at[k], dst_ref=rbuf.at[k], send_sem=send.at[k], recv_sem=recv.at[k],
        device_id={"ha": target}, device_id_type=MESH,
    )


def finish_parts(own, sbuf, rbuf, n, me, send, recv):
    total = own[...]
    for k in range(1, n):
        copy = part_copy(sbuf, rbuf, k, other(me, k), send, recv)
        copy.wait_recv()
        total = total + rbuf[k].astype(F32)
    for k in range(1, n):
        part_copy(sbuf, rbuf, k, other(me, k), send, recv).wait_send()
    return total


def ship_static(part, index, me, n, own, sbuf, rbuf, send, recv):
    for k in range(n):
        @pl.when(me == (index ^ k))
        def _(k=k):
            if k == 0:
                own[...] = part
            else:
                sbuf[k] = part.astype(BF16)
                part_copy(sbuf, rbuf, k, index, send, recv).start()


def swap_halves(values):
    width = values.shape[-1]
    lane = lax.broadcasted_iota(jnp.int32, values.shape, 1)
    half = HD // 2
    return jnp.where(
        lax.rem(lane, HD) < half,
        pltpu.roll(values, width - half, 1),
        pltpu.roll(values, half, 1),
    )


def head_masks(width, kind):
    lane = lax.broadcasted_iota(jnp.int32, (1, width), 1)
    return [(lax.div(lane, HD) == h).astype(kind) for h in range(width // HD)]


def stack_heads(block, masks):
    return jnp.concatenate([block * mask for mask in masks], axis=0)


def unstack_heads(stacked, masks, rows):
    total = None
    for h, mask in enumerate(masks):
        piece = stacked[h * rows:(h + 1) * rows] * mask
        total = piece if total is None else total + piece
    return total


def allowed_block(qdoc, kdoc, first, rows, span):
    places_q = first + lax.broadcasted_iota(jnp.int32, (rows, span), 0)
    places_k = lax.broadcasted_iota(jnp.int32, (rows, span), 1)
    return ((qdoc == kdoc) & (places_k <= places_q)) | (places_k == places_q)


def softmax_parts(scores, allowed, heads, rows):
    result = []
    for h in range(heads):
        masked = jnp.where(allowed, scores[h * rows:(h + 1) * rows] * (HD ** -0.5), -1000000000.0)
        weights = jnp.exp(masked - jnp.max(masked, axis=-1, keepdims=True))
        result.append(weights * (1.0 / jnp.sum(weights, axis=-1, keepdims=True)))
    return result


def attn_fwd_kernel(n, later, *refs):
    if later:
        (x, gain, w, cos, sin, qdoc, kdoc, first,
         middle, ng, q, k, v, att,
         wv, own, sbuf, rbuf, wsem, gs, gr, ps, pr) = refs
    else:
        (x, ng, w, cos, sin, qdoc, kdoc,
         middle, q, k, v, att, vraw,
         wv, own, sbuf, rbuf, wsem, ps, pr) = refs
    me = lax.axis_index("ha")
    rows, depth = x.shape
    width = q.shape[1]
    heads = width // HD
    greet(n, me)
    copies = [pltpu.make_async_copy(w.at[:, j], wv.at[j], wsem.at[j]) for j in range(4)]
    for copy in copies:
        copy.start()
    if later:
        ng[rows_of(me, rows)] = normalize(x[...], gain[...]).astype(BF16)
    met(n)
    if later:
        start_gather(ng, n, me, rows, gs, gr)
    for copy in copies[:3]:
        copy.wait()

    def project(block):
        where = rows_of(block, rows)
        source = ng[where]
        cosine, sine = cos[where], sin[where]
        raw = mm(source, wv[0].reshape(depth, width))
        q[where] = (raw * cosine + swap_halves(raw) * sine).astype(BF16)
        raw = mm(source, wv[1].reshape(depth, width))
        k[where] = (raw * cosine + swap_halves(raw) * sine).astype(BF16)
        raw = mm(source, wv[2].reshape(depth, width))
        if later:
            v[where] = (0.5 * raw + 0.5 * first[where]).astype(BF16)
        else:
            vraw[where] = raw
            v[where] = raw.astype(BF16)

    if later:
        project(me)
        for j in range(1, n):
            wait_block(ng, me, j, rows, gs, gr)
            project(other(me, j))
    else:
        for j in range(n):
            project(j)
    copies[3].wait()
    masks = head_masks(width, BF16)
    masks32 = head_masks(width, F32)
    for i in range(n):
        span = (i + 1) * rows
        allowed = allowed_block(qdoc[i * rows:span], kdoc[:, :span], i * rows, rows, span)
        scores = mm_nt(stack_heads(q[i * rows:span], masks), k[:span])
        probs = [p.astype(BF16) for p in softmax_parts(scores, allowed, heads, rows)]
        mixed = mm(jnp.concatenate(probs, axis=0), v[:span])
        block = unstack_heads(mixed, masks32, rows).astype(BF16)
        att[i * rows:span] = block
        ship_static(mm_nt(block, wv[3].reshape(depth, width)), i, me, n, own, sbuf, rbuf, ps, pr)
    middle[...] = x[...] + finish_parts(own, sbuf, rbuf, n, me, ps, pr)
    if later:
        wait_sent(ng, n, me, rows, gs, gr)


def ffn_fwd_kernel(n, middle, gain, w, out, ng, gate, up, wv, own, sbuf, rbuf, wsem, gs, gr, ps, pr):
    me = lax.axis_index("ha")
    rows, depth = middle.shape
    hidden = gate.shape[1]
    greet(n, me)
    copies = [pltpu.make_async_copy(w.at[:, j], wv.at[j], wsem.at[j]) for j in range(3)]
    for copy in copies:
        copy.start()
    ng[rows_of(me, rows)] = normalize(middle[...], gain[...]).astype(BF16)
    met(n)
    start_gather(ng, n, me, rows, gs, gr)
    for copy in copies:
        copy.wait()

    def branch(block):
        where = rows_of(block, rows)
        source = ng[where]
        g = mm(source, wv[0].reshape(depth, hidden))
        u = mm(source, wv[1].reshape(depth, hidden))
        gate[where] = g
        up[where] = u
        return mm_nt((g * jax.nn.sigmoid(g) * u).astype(BF16), wv[2].reshape(depth, hidden))

    own[...] = branch(me)
    for k in range(1, n):
        wait_block(ng, me, k, rows, gs, gr)
        sbuf[k] = branch(other(me, k)).astype(BF16)
        part_copy(sbuf, rbuf, k, other(me, k), ps, pr).start()
    out[...] = middle[...] + finish_parts(own, sbuf, rbuf, n, me, ps, pr)
    wait_sent(ng, n, me, rows, gs, gr)


def ffn_back_kernel(n, turn, *refs):
    if turn:
        (middle, gain, w, gy, gg,
         gmiddle, ggain, dw, ypart,
         ng, hid, ggate, gup, wv, own, sbuf, rbuf, wsem, gs, gr, ps, pr) = refs
    else:
        (middle, gain, w, gy, ng, gate_hbm, up_hbm,
         gmiddle, ggain, dw,
         gate, up, gg, hid, ggate, gup, wv, own, sbuf, rbuf, wsem, gs, gr, ps, pr) = refs
    me = lax.axis_index("ha")
    rows, depth = middle.shape
    hidden = hid.shape[1]
    greet(n, me)
    copies = [pltpu.make_async_copy(w.at[:, j], wv.at[j], wsem.at[j]) for j in range(3)]
    if not turn:
        copies.append(pltpu.make_async_copy(gate_hbm, gate, wsem.at[3]))
        copies.append(pltpu.make_async_copy(up_hbm, up, wsem.at[4]))
    for copy in copies:
        copy.start()
    if turn:
        moving = ng
        ng[rows_of(me, rows)] = normalize(middle[...], gain[...]).astype(BF16)
    else:
        moving = gg
        gg[rows_of(me, rows)] = gy[...].astype(BF16)
    met(n)
    start_gather(moving, n, me, rows, gs, gr)
    for copy in copies:
        copy.wait()

    def branch(block):
        where = rows_of(block, rows)
        if turn:
            source = ng[where]
            g = mm(source, wv[0].reshape(depth, hidden))
            u = mm(source, wv[1].reshape(depth, hidden))
        else:
            g, u = gate[where], up[where]
        s = jax.nn.sigmoid(g)
        h = (g * s * u).astype(BF16)
        hid[where] = h
        if turn:
            ypart[where] = mm_nt(h, wv[2].reshape(depth, hidden)).astype(BF16)
        gh = mm(gg[where], wv[2].reshape(depth, hidden))
        a = (gh * u * s * (1.0 + g * (1.0 - s))).astype(BF16)
        b = (gh * g * s).astype(BF16)
        ggate[where] = a
        gup[where] = b
        return mm_nt(a, wv[0].reshape(depth, hidden)) + mm_nt(b, wv[1].reshape(depth, hidden))

    own[...] = branch(me)
    for k in range(1, n):
        wait_block(moving, me, k, rows, gs, gr)
        sbuf[k] = branch(other(me, k)).astype(BF16)
        part_copy(sbuf, rbuf, k, other(me, k), ps, pr).start()
    shape = (w.shape[0], w.shape[2], hidden)
    dw[:, 0] = mm_tn(ng[...], ggate[...]).astype(BF16).reshape(shape)
    dw[:, 1] = mm_tn(ng[...], gup[...]).astype(BF16).reshape(shape)
    dw[:, 2] = mm_tn(gg[...], hid[...]).astype(BF16).reshape(shape)
    total = finish_parts(own, sbuf, rbuf, n, me, ps, pr)
    back, gain_part = norm_back(middle[...], gain[...], total)
    gmiddle[...] = gy[...].astype(F32) + back
    ggain[...] = gain_part
    wait_sent(moving, n, me, rows, gs, gr)


def attn_back_kernel(n, later, *refs):
    if later:
        (x, gain, w, gmid, ng, q, k, v, att, cos, sin, qdoc, kdoc,
         gx, ggain, dw, carry,
         gg, gat, gq, gk, gv, gka, gva, wv, own, sbuf, rbuf, wsem, gs, gr, ps, pr) = refs
    else:
        (x, gain, w, gmid, ng, q, k, v, att, cos, sin, qdoc, kdoc, carry,
         gx, ggain, dw,
         gg, gat, gq, gk, gv, gka, gva, wv, own, sbuf, rbuf, wsem, gs, gr, ps, pr) = refs
    me = lax.axis_index("ha")
    rows, depth = x.shape
    width = q.shape[1]
    heads = width // HD
    greet(n, me)
    copies = [pltpu.make_async_copy(w.at[:, j], wv.at[j], wsem.at[j]) for j in range(4)]
    for copy in copies:
        copy.start()
    gg[rows_of(me, rows)] = gmid[...].astype(BF16)
    met(n)
    start_gather(gg, n, me, rows, gs, gr)
    gka[...] = jnp.zeros_like(gka)
    gva[...] = jnp.zeros_like(gva)
    for copy in copies:
        copy.wait()

    def pull(block):
        where = rows_of(block, rows)
        gat[where] = mm(gg[where], wv[3].reshape(depth, width)).astype(BF16)

    pull(me)
    for j in range(1, n):
        wait_block(gg, me, j, rows, gs, gr)
        pull(other(me, j))
    masks = head_masks(width, BF16)
    masks32 = head_masks(width, F32)
    for i in reversed(range(n)):
        span = (i + 1) * rows
        here = slice(i * rows, span)
        allowed = allowed_block(qdoc[here], kdoc[:, :span], i * rows, rows, span)
        qs = stack_heads(q[here], masks)
        gas = stack_heads(gat[here], masks)
        probs = softmax_parts(mm_nt(qs, k[:span]), allowed, heads, rows)
        gprobs = mm_nt(gas, v[:span])
        raws = []
        for h in range(heads):
            p = probs[h]
            gp = gprobs[h * rows:(h + 1) * rows]
            inner = jnp.sum(p * gp, axis=-1, keepdims=True)
            raws.append((p * (gp - inner) * (HD ** -0.5)).astype(BF16))
        raw = jnp.concatenate(raws, axis=0)
        low = jnp.concatenate([p.astype(BF16) for p in probs], axis=0)
        gva[:span] += mm_tn(low, gas)
        gka[:span] += mm_tn(raw, qs)
        cosine, sine = cos[here], sin[here]
        gqr = unstack_heads(mm(raw, k[:span]), masks32, rows)
        gqr = (gqr * cosine - swap_halves(gqr) * sine).astype(BF16)
        gkr = gka[here]
        gkr = (gkr * cosine - swap_halves(gkr) * sine).astype(BF16)
        if later:
            half = 0.5 * gva[here]
            carry[here] = half
            gvr = half.astype(BF16)
        else:
            gvr = (gva[here] + carry[here]).astype(BF16)
        gq[here] = gqr
        gk[here] = gkr
        gv[here] = gvr
        part = (
            mm_nt(gqr, wv[0].reshape(depth, width))
            + mm_nt(gkr, wv[1].reshape(depth, width))
            + mm_nt(gvr, wv[2].reshape(depth, width))
        )
        ship_static(part, i, me, n, own, sbuf, rbuf, ps, pr)
    shape = (w.shape[0], w.shape[2], width)
    dw[:, 3] = mm_tn(gg[...], att[...]).astype(BF16).reshape(shape)
    dw[:, 0] = mm_tn(ng[...], gq[...]).astype(BF16).reshape(shape)
    dw[:, 1] = mm_tn(ng[...], gk[...]).astype(BF16).reshape(shape)
    dw[:, 2] = mm_tn(ng[...], gv[...]).astype(BF16).reshape(shape)
    total = finish_parts(own, sbuf, rbuf, n, me, ps, pr)
    back, gain_part = norm_back(x[...], gain[...], total)
    gx[...] = gmid[...] + back
    ggain[...] = gain_part
    wait_sent(gg, n, me, rows, gs, gr)


def gains_kernel(n, g, parts, out, abuf, bbuf, asend, arecv, bsend, brecv):
    ha = lax.axis_index("ha")
    af = lax.axis_index("af")
    barrier = pltpu.get_barrier_semaphore()
    for k in range(1, n):
        pl.semaphore_signal(barrier, inc=1, device_id={"ha": other(ha, k)}, device_id_type=MESH)
    for k in range(1, g):
        pl.semaphore_signal(barrier, inc=1, device_id={"af": other(af, k)}, device_id_type=MESH)
    pl.semaphore_wait(barrier, n + g - 2)

    def exchange(axis, me, count, buffer, send, recv):
        copies = []
        for k in range(1, count):
            copies.append(pltpu.make_async_remote_copy(
                src_ref=buffer.at[me], dst_ref=buffer.at[me], send_sem=send.at[k], recv_sem=recv.at[k],
                device_id={axis: other(me, k)}, device_id_type=MESH,
            ))
            copies[-1].start()
        for k in range(1, count):
            theirs = buffer.at[other(me, k)]
            pltpu.make_async_remote_copy(
                src_ref=theirs, dst_ref=theirs, send_sem=send.at[k], recv_sem=recv.at[k],
                device_id={axis: other(me, k)}, device_id_type=MESH,
            ).wait_recv()
        total = buffer[0]
        for j in range(1, count):
            total = total + buffer[j]
        for copy in copies:
            copy.wait_send()
        return total

    abuf[ha] = parts[...]
    bbuf[af] = exchange("ha", ha, n, abuf, asend, arecv)
    out[...] = exchange("af", af, g, bbuf, bsend, brecv)


def sems(count):
    return pltpu.SemaphoreType.DMA((count,))


def traffic(n, rows, depth):
    return [
        pltpu.VMEM((rows, depth), F32),
        pltpu.VMEM((n, rows, depth), BF16),
        pltpu.VMEM((n, rows, depth), BF16),
    ]


def launch(kernel, name, number, args, in_any, outs, scratch, flops):
    return pl.pallas_call(
        kernel,
        out_shape=outs,
        in_specs=[ANY if j in in_any else VMEM for j in range(len(args))],
        out_specs=[VMEM] * len(outs),
        scratch_shapes=scratch,
        compiler_params=pltpu.CompilerParams(
            collective_id=number, has_side_effects=True, vmem_limit_bytes=48 * 1024 * 1024
        ),
        cost_estimate=pl.CostEstimate(flops=flops, bytes_accessed=16 * 1024 * 1024, transcendentals=0),
        name=name,
    )(*args)


def per_device(
    block_input, lengths, cotangent,
    attngain_early, query_early, keys_early, values_early, output_early,
    ffngain_early, gate_early, upward_early, down_early,
    attngain_later, query_later, keys_later, values_later, output_later,
    ffngain_later, gate_later, upward_later, down_later,
):
    n, g = lax.axis_size("ha"), lax.axis_size("af")
    rows, depth = block_input.shape
    bucket = rows * n
    wrows, width = query_early.shape
    hidden = gate_early.shape[1]
    shape = jax.ShapeDtypeStruct
    cos, sin, qdoc, kdoc = layout(lengths[0], bucket, width // HD)

    def gather(*matrices):
        return lax.all_gather(jnp.stack(matrices), "af", axis=0, tiled=False)

    x = block_input.astype(F32)
    gain_rows = [v[None, :] for v in (attngain_early, ffngain_early, attngain_later, ffngain_later)]
    attn_early = gather(query_early, keys_early, values_early, output_early)
    ng1 = lax.all_gather(normalize(x, gain_rows[0]).astype(BF16), "ha", axis=0, tiled=True)
    ffn_early = gather(gate_early, upward_early, down_early)
    attn_later = gather(query_later, keys_later, values_later, output_later)
    cot = lax.all_gather(cotangent, "ha", axis=0, tiled=True)
    ffn_later = gather(gate_later, upward_later, down_later)

    tokens16 = shape((bucket, depth), BF16)
    heads16 = shape((bucket, width), BF16)
    heads32 = shape((bucket, width), F32)
    own32 = shape((rows, depth), F32)
    gain32 = shape((1, depth), F32)
    wide = pltpu.VMEM((bucket, hidden), BF16)
    tall = pltpu.VMEM((bucket, depth), BF16)
    slim = pltpu.VMEM((bucket, width), BF16)
    slim32 = pltpu.VMEM((bucket, width), F32)
    attn_w = pltpu.VMEM((4, g, wrows, width), BF16)
    ffn_w = pltpu.VMEM((3, g, wrows, hidden), BF16)
    moves = traffic(n, rows, depth)
    attn_flops = 2 * bucket * depth * width * 4
    ffn_flops = 2 * bucket * depth * hidden * 3

    middle1, q1, k1, v1, att1, vraw1 = launch(
        functools.partial(attn_fwd_kernel, n, False), "attn_fwd_early", 1,
        [x, ng1, attn_early, cos, sin, qdoc, kdoc], (2,),
        [own32, heads16, heads16, heads16, heads16, heads32],
        [attn_w, *moves, sems(4), sems(n), sems(n)], attn_flops,
    )
    out1, ng2, gate1, up1 = launch(
        functools.partial(ffn_fwd_kernel, n), "ffn_fwd_early", 2,
        [middle1, gain_rows[1], ffn_early], (2,),
        [own32, tokens16, shape((bucket, hidden), F32), shape((bucket, hidden), F32)],
        [ffn_w, *moves, sems(3), sems(n), sems(n), sems(n), sems(n)], ffn_flops,
    )
    middle2, ng3, q2, k2, v2, att2 = launch(
        functools.partial(attn_fwd_kernel, n, True), "attn_fwd_later", 3,
        [out1, gain_rows[2], attn_later, cos, sin, qdoc, kdoc, vraw1], (2,),
        [own32, tokens16, heads16, heads16, heads16, heads16],
        [attn_w, *moves, sems(4), sems(n), sems(n), sems(n), sems(n)], attn_flops,
    )
    gmid2, ffngain2, dffn2, ypart = launch(
        functools.partial(ffn_back_kernel, n, True), "ffn_turn_later", 4,
        [middle2, gain_rows[3], ffn_later, cotangent, cot], (2,),
        [own32, gain32, shape((g, 3, wrows, hidden), BF16), tokens16],
        [tall, wide, wide, wide, ffn_w, *moves, sems(3), sems(n), sems(n), sems(n), sems(n)], 3 * ffn_flops,
    )
    gout1, attngain2, dattn2, carry = launch(
        functools.partial(attn_back_kernel, n, True), "attn_back_later", 5,
        [out1, gain_rows[2], attn_later, gmid2, ng3, q2, k2, v2, att2, cos, sin, qdoc, kdoc], (2,),
        [own32, gain32, shape((g, 4, wrows, width), BF16), heads32],
        [tall, slim, slim, slim, slim, slim32, slim32, attn_w, *moves,
         sems(4), sems(n), sems(n), sems(n), sems(n)], 2 * attn_flops,
    )
    gmid1, ffngain1, dffn1 = launch(
        functools.partial(ffn_back_kernel, n, False), "ffn_back_early", 6,
        [middle1, gain_rows[1], ffn_early, gout1, ng2, gate1, up1], (2, 5, 6),
        [own32, gain32, shape((g, 3, wrows, hidden), BF16)],
        [pltpu.VMEM((bucket, hidden), F32), pltpu.VMEM((bucket, hidden), F32),
         tall, wide, wide, wide, ffn_w, *moves, sems(5), sems(n), sems(n), sems(n), sems(n)], 2 * ffn_flops,
    )
    grads, attngain1, dattn1 = launch(
        functools.partial(attn_back_kernel, n, False), "attn_back_early", 7,
        [x, gain_rows[0], attn_early, gmid1, ng1, q1, k1, v1, att1, cos, sin, qdoc, kdoc, carry], (2,),
        [own32, gain32, shape((g, 4, wrows, width), BF16)],
        [tall, slim, slim, slim, slim, slim32, slim32, attn_w, *moves,
         sems(4), sems(n), sems(n), sems(n), sems(n)], 2 * attn_flops,
    )

    def scatter(partial_sums):
        return lax.psum_scatter(partial_sums, "af", scatter_dimension=0, tiled=False).astype(F32)

    block_output = (
        middle2 + lax.psum_scatter(ypart, "ha", scatter_dimension=0, tiled=True).astype(F32)
    ).astype(BF16)
    fl, al, fe, ae = scatter(dffn2), scatter(dattn2), scatter(dffn1), scatter(dattn1)
    parts = jnp.concatenate([attngain1, ffngain1, attngain2, ffngain2], axis=0)
    gains, = launch(
        functools.partial(gains_kernel, n, g), "gain_sums", 8, [parts], (), [shape(parts.shape, F32)],
        [pltpu.VMEM((n, *parts.shape), F32), pltpu.VMEM((g, *parts.shape), F32),
         sems(n), sems(n), sems(g), sems(g)], 0,
    )
    return (
        block_output, grads,
        gains[0], ae[0], ae[1], ae[2], ae[3], gains[1], fe[0], fe[1], fe[2],
        gains[2], al[0], al[1], al[2], al[3], gains[3], fl[0], fl[1], fl[2],
    )


def solution(mesh):
    tokens = P(("af", "ha"), None)
    matrix = P("af", "ha")
    layer = (P(), matrix, matrix, matrix, matrix, P(), matrix, matrix, matrix)
    return jax.shard_map(
        per_device, mesh=mesh,
        in_specs=(tokens, P("af", None), tokens, *layer, *layer),
        out_specs=(tokens, tokens, *layer, *layer),
        check_vma=False,
    )
```

```python
import functools
import types

import jax
import jax.numpy as jnp
import numpy as np
from jax import lax
from jax.experimental import pallas as pl
from jax.experimental.pallas import tpu as pltpu
from jax.sharding import PartitionSpec as P

HD = 64
epsilon = 1e-06
rope_base = 10000.0
MESH = pl.DeviceIdType.MESH
VMEM = pl.BlockSpec(memory_space=pltpu.VMEM)
ANY = pl.BlockSpec(memory_space=pl.ANY)
F32 = jnp.float32
BF16 = jnp.bfloat16


def mm(left, right):
    return jnp.dot(left, right, preferred_element_type=F32)


def mm_nt(left, right):
    return lax.dot_general(left, right, (((1,), (1,)), ((), ())), preferred_element_type=F32)


def mm_tn(left, right):
    return lax.dot_general(left, right, (((0,), (0,)), ((), ())), preferred_element_type=F32)


def normalize(values, gain):
    return values * lax.rsqrt(jnp.mean(values * values, axis=-1, keepdims=True) + epsilon) * gain


def norm_back(values, gain, grads):
    scaling = lax.rsqrt(jnp.mean(values * values, axis=-1, keepdims=True) + epsilon)
    weighted = gain * grads
    inner = jnp.mean(weighted * values, axis=-1, keepdims=True)
    return (
        scaling * weighted - values * scaling * scaling * scaling * inner,
        jnp.sum(grads * values * scaling, axis=0, keepdims=True),
    )


def other(me, k):
    result, bit = me, 1
    while bit <= k:
        if k & bit:
            result = result + bit * (1 - 2 * lax.rem(lax.div(me, bit), 2))
        bit *= 2
    return result


def swap_halves(values):
    width = values.shape[-1]
    lane = lax.broadcasted_iota(jnp.int32, values.shape, 1)
    half = HD // 2
    return jnp.where(
        lax.rem(lane, HD) < half,
        pltpu.roll(values, width - half, 1),
        pltpu.roll(values, half, 1),
    )


def head_masks(width, kind):
    lane = lax.broadcasted_iota(jnp.int32, (1, width), 1)
    return [(lax.div(lane, HD) == h).astype(kind) for h in range(width // HD)]


def stack_heads(block, masks):
    return jnp.concatenate([block * mask for mask in masks], axis=0)


def unstack_heads(stacked, masks, rows):
    total = None
    for h, mask in enumerate(masks):
        piece = stacked[h * rows:(h + 1) * rows] * mask
        total = piece if total is None else total + piece
    return total


def softmax_parts(scores, allowed, heads, rows):
    result = []
    for h in range(heads):
        masked = jnp.where(allowed, scores[h * rows:(h + 1) * rows] * (HD ** -0.5), -1000000000.0)
        weights = jnp.exp(masked - jnp.max(masked, axis=-1, keepdims=True))
        result.append(weights * (1.0 / jnp.sum(weights, axis=-1, keepdims=True)))
    return result


def rows_of(index, count):
    return pl.ds(pl.multiple_of(index * count, count), count)


def remote(source, target, send, recv, **place):
    return pltpu.make_async_remote_copy(
        src_ref=source, dst_ref=target, send_sem=send, recv_sem=recv, device_id=place, device_id_type=MESH
    )


class Step:
    def __init__(self, n, g, refs):
        self.n, self.g, self.zs = n, g, g // 2
        self.r = refs
        self.ha, self.af = lax.axis_index("ha"), lax.axis_index("af")
        self.z, self.c = lax.div(self.af, 2), lax.rem(self.af, 2)
        self.sibling = self.af + 1 - 2 * self.c
        self.rows, self.depth = refs.x.shape
        self.bucket = self.rows * n
        self.width = refs.q[0].shape[1]
        self.heads = self.width // HD
        self.hidden = refs.gate.shape[1]
        self.count = self.depth // g
        self.flip = refs.w[1].shape[3] == self.count
        self.ends = self.zs > 3
        self.reach = self.zs - 2 if self.ends else self.zs - 1


    def token_copy(self, buffer, slot, owner, k):
        block = buffer.at[rows_of(owner, self.rows)]
        return remote(block, block, self.r.ags.at[slot, k], self.r.agr.at[slot, k], ha=other(self.ha, k))

    def spread(self, buffer, slot):
        for k in range(1, self.n):
            self.token_copy(buffer, slot, self.ha, k).start()

    def arrived(self, buffer, slot, k):
        self.token_copy(buffer, slot, other(self.ha, k), k).wait_recv()

    def spread_done(self, buffer, slot):
        for k in range(1, self.n):
            self.token_copy(buffer, slot, self.ha, k).wait_send()

    def part_copy(self, slot, k, target):
        return remote(self.r.sbuf.at[k], self.r.rbuf.at[k], self.r.pss.at[slot, k], self.r.psr.at[slot, k], ha=target)

    def ship(self, part, slot, index):
        for k in range(self.n):
            @pl.when(self.ha == (index ^ k))
            def _(k=k):
                if k == 0:
                    self.r.own[...] = part
                else:
                    self.r.sbuf[k] = part.astype(BF16)
                    self.part_copy(slot, k, index).start()

    def collect(self, slot):
        total = self.r.own[...]
        for k in range(1, self.n):
            self.part_copy(slot, k, other(self.ha, k)).wait_recv()
            total = total + self.r.rbuf[k].astype(F32)
        for k in range(1, self.n):
            self.part_copy(slot, k, other(self.ha, k)).wait_send()
        return total

    def output_copy(self, k):
        target = other(self.ha, k)
        return remote(
            self.r.ypart.at[rows_of(target, self.rows)], self.r.yrecv.at[k],
            self.r.pss.at[7, k], self.r.psr.at[7, k], ha=target,
        )


    def block(self, i, z, c):
        return self.r.w[i].at[z * 2 + c]

    def local_copy(self, i, j):
        return pltpu.make_async_copy(self.r.whbm[i, j], self.r.w[i].at[self.af, j], self.r.lsem.at[i, j])

    def to_sibling(self, i, z):
        block = self.block(i, z, self.c)
        return remote(block, block, self.r.gs.at[i, 0, z], self.r.gr.at[i, 0, z], af=self.sibling)

    def along(self, i, source, z, slot):
        block = self.block(i, source, self.c)
        return remote(block, block, self.r.gs.at[i, 1, slot], self.r.gr.at[i, 1, source], af=z * 2 + self.c)

    def neighbours(self, do, far_first=False):
        distances = range(1, self.reach + 1)
        for d in reversed(distances) if far_first else distances:
            for t in (self.z + d, self.z - d):
                pl.when((t >= 0) & (t < self.zs))(functools.partial(do, t))

    def gather_start(self, i):
        for j in range(self.r.w[i].shape[1]):
            self.local_copy(i, j).wait()
        self.neighbours(lambda t: self.along(i, self.z, t, t).start(), far_first=True)
        self.to_sibling(i, self.z).start()

    def gather_mid(self, i):
        last = self.zs - 1

        def take(t):
            self.along(i, t, t, t).wait_recv()
            self.to_sibling(i, t).start()

        self.neighbours(take)
        if self.ends:
            pl.when(self.z == last - 1)(lambda: self.along(i, 0, last, last + 1).start())
            pl.when(self.z == 1)(lambda: self.along(i, last, 0, last + 2).start())

    def gather_end(self, i):
        last = self.zs - 1

        def take(t):
            self.along(i, t, t, t).wait_recv()
            self.to_sibling(i, t).start()

        if self.ends:
            pl.when(self.z == last)(functools.partial(take, 0))
            pl.when(self.z == 0)(functools.partial(take, last))
        for t in range(self.zs):
            block = self.block(i, t, 1 - self.c)
            remote(block, block, self.r.gs.at[i, 0, t], self.r.gr.at[i, 0, t], af=self.sibling).wait_recv()

    def gather_drain(self, i):
        last = self.zs - 1
        self.neighbours(lambda t: self.along(i, self.z, t, t).wait_send())
        for t in range(self.zs):
            self.to_sibling(i, t).wait_send()
        if self.ends:
            pl.when(self.z == last - 1)(lambda: self.along(i, 0, last, last + 1).wait_send())
            pl.when(self.z == 1)(lambda: self.along(i, last, 0, last + 2).wait_send())


    def swap_copy(self, i):
        return remote(
            self.r.part[i % 2].at[1 - self.c], self.r.swapped[i % 2], self.r.rs.at[i, 0], self.r.rr.at[i, 0],
            af=self.sibling,
        )

    def sum_copy(self, i, source, z):
        return remote(
            self.r.part[i % 2].at[self.c, z], self.r.zrecv[i].at[source],
            self.r.rs.at[i, 1 + z], self.r.rr.at[i, 1 + source], af=z * 2 + self.c,
        )

    def merge_copy(self, i, up):
        last = self.zs - 1
        block, target = (last, 1) if up else (0, last - 1)
        slot = self.zs + (1 if up else 2)
        return remote(
            self.r.part[i % 2].at[self.c, block], self.r.zrecv[i].at[target],
            self.r.rs.at[i, slot], self.r.rr.at[i, slot], af=target * 2 + self.c,
        )

    def reduce_start(self, i):
        self.swap_copy(i).start()

    def reduce_mid(self, i):
        part, swapped, last = self.r.part[i % 2], self.r.swapped[i % 2], self.zs - 1
        self.swap_copy(i).wait_recv()

        def add(t, carry):
            part[self.c, t] = (part[self.c, t].astype(F32) + swapped[t].astype(F32)).astype(BF16)
            return carry

        lax.fori_loop(0, self.zs, add, 0)
        if self.ends:
            pl.when(self.z == 0)(lambda: self.merge_copy(i, True).start())
            pl.when(self.z == last)(lambda: self.merge_copy(i, False).start())

        def send(t):
            if self.ends:
                held = ((self.z == 1) & (t == last)) | ((self.z == last - 1) & (t == 0))
                pl.when(jnp.logical_not(held))(lambda: self.sum_copy(i, self.z, t).start())
            else:
                self.sum_copy(i, self.z, t).start()

        self.neighbours(send, far_first=True)

    def reduce_merge(self, i):
        part, last = self.r.part[i % 2], self.zs - 1
        if self.ends:
            def merge(up):
                block = last if up else 0
                self.merge_copy(i, up).wait_recv()
                part[self.c, block] = (
                    part[self.c, block].astype(F32) + self.r.zrecv[i][1 if up else last - 1].astype(F32)
                ).astype(BF16)
                self.sum_copy(i, self.z, block).start()

            pl.when(self.z == 1)(functools.partial(merge, True))
            pl.when(self.z == last - 1)(functools.partial(merge, False))

    def reduce_end(self, i):
        part, out, last = self.r.part[i % 2], self.r.sums[i], self.zs - 1
        out[...] = part[self.c, self.z].astype(F32)

        def take(t):
            self.sum_copy(i, t, t).wait_recv()
            out[...] += self.r.zrecv[i][t].astype(F32)

        self.neighbours(take)
        self.swap_copy(i).wait_send()
        self.neighbours(lambda t: self.sum_copy(i, self.z, t).wait_send())
        if self.ends:
            pl.when(self.z == 0)(lambda: self.merge_copy(i, True).wait_send())
            pl.when(self.z == last)(lambda: self.merge_copy(i, False).wait_send())

    def products(self, i, pairs):
        part, count = self.r.part[i % 2], self.count

        def chip(z, carry):
            here = pl.ds(pl.multiple_of(z * 2 * count, 2 * count), 2 * count)
            for j, left, right in pairs:
                if i % 2 == 0 and self.flip:
                    product = mm(right[...], left[:, here]).astype(BF16)
                    part[0, z, j] = product[:, :count]
                    part[1, z, j] = product[:, count:]
                else:
                    product = mm_tn(left[:, here], right[...]).astype(BF16)
                    part[0, z, j] = product[:count]
                    part[1, z, j] = product[count:]
            return carry

        lax.fori_loop(0, self.zs, chip, 0)


    def tables(self):
        r = self.r
        count = r.lengths.shape[1]
        places = lax.broadcasted_iota(jnp.int32, (self.bucket, 1), 0)
        beginning = jnp.zeros((self.bucket, 1), jnp.int32)
        end = 0
        for s in range(count):
            start, end = end, end + r.lengths[0, s]
            beginning = jnp.where((places >= start) & (places < end), start, beginning)
        angles = (places - beginning).astype(F32) * r.wave[0:1]
        r.cos[...] = jnp.cos(angles)
        r.sin[...] = jnp.sin(angles) * r.wave[1:2]

    def turning(self, where):
        copies = self.width // 128
        return (
            jnp.concatenate([self.r.cos[where]] * copies, axis=1),
            jnp.concatenate([self.r.sin[where]] * copies, axis=1),
        )

    def allowed(self, i):
        span = (i + 1) * self.rows
        places_q = i * self.rows + lax.broadcasted_iota(jnp.int32, (self.rows, 1), 0)
        places_k = lax.broadcasted_iota(jnp.int32, (1, span), 1)
        qdoc = jnp.zeros((self.rows, 1), jnp.int32)
        kdoc = jnp.zeros((1, span), jnp.int32)
        end = 0
        for s in range(self.r.lengths.shape[1]):
            end = end + self.r.lengths[0, s]
            qdoc = qdoc + (places_q >= end).astype(jnp.int32)
            kdoc = kdoc + (places_k >= end).astype(jnp.int32)
        qdoc = jnp.where(places_q >= end, -1, qdoc)
        return ((qdoc == kdoc) & (places_k <= places_q)) | (places_k == places_q)

    def matrix(self, i, j):
        return self.r.w[i][:, j].reshape(self.depth, self.r.w[i].shape[-1])

    def turned(self, i, j):
        return jnp.concatenate([self.r.w[i][owner, j] for owner in range(self.g)], axis=1)

    def into_hidden(self, source, i, j):
        return mm_nt(source, self.turned(i, j)) if self.flip else mm(source, self.matrix(i, j))

    def out_of_hidden(self, source, i, j):
        return mm(source, self.turned(i, j)) if self.flip else mm_nt(source, self.matrix(i, j))


    def project(self, layer, block):
        r = self.r
        where = rows_of(block, self.rows)
        source = r.ng[2 * layer][where]
        cosine, sine = self.turning(where)
        raw = mm(source, self.matrix(3 * layer, 0))
        r.q[layer][where] = (raw * cosine + swap_halves(raw) * sine).astype(BF16)
        raw = mm(source, self.matrix(3 * layer, 1))
        r.k[layer][where] = (raw * cosine + swap_halves(raw) * sine).astype(BF16)
        raw = mm(source, self.matrix(3 * layer, 2))
        if layer == 0:
            r.first[where] = raw
            r.v[layer][where] = raw.astype(BF16)
        else:
            r.v[layer][where] = (0.5 * raw + 0.5 * r.first[where]).astype(BF16)

    def attend(self, layer, slot):
        r, rows = self.r, self.rows
        masks, masks32 = head_masks(self.width, BF16), head_masks(self.width, F32)
        for i in range(self.n):
            span = (i + 1) * rows
            here = slice(i * rows, span)
            scores = mm_nt(stack_heads(r.q[layer][here], masks), r.k[layer][:span])
            probs = [p.astype(BF16) for p in softmax_parts(scores, self.allowed(i), self.heads, rows)]
            mixed = mm(jnp.concatenate(probs, axis=0), r.v[layer][:span])
            block = unstack_heads(mixed, masks32, rows).astype(BF16)
            r.att[layer][here] = block
            self.ship(mm_nt(block, self.matrix(3 * layer, 3)), slot, i)

    def attend_back(self, layer, slot):
        r, rows = self.r, self.rows
        masks, masks32 = head_masks(self.width, BF16), head_masks(self.width, F32)
        scale = HD ** -0.5
        for i in reversed(range(self.n)):
            span = (i + 1) * rows
            here = slice(i * rows, span)
            keys, vals = r.k[layer][:span], r.v[layer][:span]
            qs = stack_heads(r.q[layer][here], masks)
            gas = stack_heads(r.gat[here], masks)
            probs = softmax_parts(mm_nt(qs, keys), self.allowed(i), self.heads, rows)
            gprobs = mm_nt(gas, vals)
            raws = []
            for h in range(self.heads):
                p, gp = probs[h], gprobs[h * rows:(h + 1) * rows]
                inner = jnp.sum(p * gp, axis=-1, keepdims=True)
                raws.append((p * (gp - inner) * scale).astype(BF16))
            raw = jnp.concatenate(raws, axis=0)
            low = jnp.concatenate([p.astype(BF16) for p in probs], axis=0)
            if i == self.n - 1:
                r.gva[...] = mm_tn(low, gas)
                r.gka[...] = mm_tn(raw, qs)
            else:
                r.gva[:span] += mm_tn(low, gas)
                r.gka[:span] += mm_tn(raw, qs)
            cosine, sine = self.turning(here)
            gqr = unstack_heads(mm(raw, keys), masks32, rows)
            gqr = (gqr * cosine - swap_halves(gqr) * sine).astype(BF16)
            gkr = r.gka[here]
            gkr = (gkr * cosine - swap_halves(gkr) * sine).astype(BF16)
            if layer == 1:
                half = 0.5 * r.gva[here]
                r.carry[here] = half
                gvr = half.astype(BF16)
            else:
                gvr = (r.gva[here] + r.carry[here]).astype(BF16)
            r.gq[here], r.gk[here], r.gv[here] = gqr, gkr, gvr
            part = (
                mm_nt(gqr, self.matrix(3 * layer, 0))
                + mm_nt(gkr, self.matrix(3 * layer, 1))
                + mm_nt(gvr, self.matrix(3 * layer, 2))
            )
            self.ship(part, slot, i)

    def feed(self, layer, slot, buffer, agslot, turn, ready):
        r = self.r

        def first(where):
            source = r.ng[2 * layer + 1][where]
            g = self.into_hidden(source, 3 * layer + 1, 0)
            u = self.into_hidden(source, 3 * layer + 1, 1)
            if not turn:
                r.gate[where], r.up[where] = g, u
            return g, u

        def second(where, g, u):
            if not turn:
                return self.out_of_hidden((g * jax.nn.sigmoid(g) * u).astype(BF16), 3 * layer + 2, 0)
            part, h = self.feed_back(layer, where, 0, g, u)
            r.ypart[where] = self.out_of_hidden(h, 3 * layer + 2, 0).astype(BF16)
            return part

        mine = rows_of(self.ha, self.rows)
        g, u = first(mine)
        ready()
        r.own[...] = second(mine, g, u)
        for k in range(1, self.n):
            self.arrived(buffer, agslot, k)
            where = rows_of(other(self.ha, k), self.rows)
            r.sbuf[k] = second(where, *first(where)).astype(BF16)
            self.part_copy(slot, k, other(self.ha, k)).start()

    def feed_back(self, layer, where, gg, g, u):
        r = self.r
        s = jax.nn.sigmoid(g)
        h = (g * s * u).astype(BF16)
        gh = self.into_hidden(r.gg[gg][where], 3 * layer + 2, 0)
        a = (gh * u * s * (1.0 + g * (1.0 - s))).astype(BF16)
        b = (gh * g * s).astype(BF16)
        for j, value in enumerate((a, b, h)):
            if self.flip:
                r.units[j][:, where] = value.T
            else:
                r.units[j][where] = value
        return self.out_of_hidden(a, 3 * layer + 1, 0) + self.out_of_hidden(b, 3 * layer + 1, 1), h

    def feed_grads(self, layer):
        r = self.r
        normed = r.ng[2 * layer + 1]
        self.products(2 * layer, [(0, normed, r.units[0]), (1, normed, r.units[1]), (2, r.gg[0], r.units[2])])

    def attend_grads(self, layer):
        r = self.r
        normed = r.ng[2 * layer]
        self.products(2 * layer + 1, [(0, normed, r.gq), (1, normed, r.gk), (2, normed, r.gv), (3, r.gg[1], r.att[layer])])


    def gain_phase(self, slot, axis, me, count, place):
        buffer = self.r.gbuf[slot]
        for t in range(count):
            copy = remote(
                buffer.at[me], buffer.at[me], self.r.gns.at[slot, t], self.r.gnr.at[slot, me], **{axis: place(t)}
            )
            pl.when(me != t)(copy.start)

    def gain_sum(self, slot, axis, me, count, place):
        buffer = self.r.gbuf[slot]
        for t in range(count):
            copy = remote(
                buffer.at[t], buffer.at[t], self.r.gns.at[slot, t], self.r.gnr.at[slot, t], **{axis: place(t)}
            )
            pl.when(me != t)(copy.wait)
        total = buffer[0]
        for t in range(1, count):
            total = total + buffer[t]
        return total

    def run(self):
        r, n = self.r, self.n
        barrier = pltpu.get_barrier_semaphore()
        for k in range(1, n):
            pl.semaphore_signal(barrier, inc=1, device_id={"ha": other(self.ha, k)}, device_id_type=MESH)
        pl.semaphore_signal(barrier, inc=1, device_id={"af": self.sibling}, device_id_type=MESH)
        for d in range(1, self.zs):
            t = lax.rem(self.z + d, self.zs)
            pl.semaphore_signal(barrier, inc=1, device_id={"af": t * 2 + self.c}, device_id_type=MESH)
        for i in range(6):
            for j in range(r.w[i].shape[1]):
                self.local_copy(i, j).start()
        mine = rows_of(self.ha, self.rows)
        x = r.x[...].astype(F32)
        r.ng[0][mine] = normalize(x, r.gains[0][...]).astype(BF16)
        r.gg[0][mine] = r.cot[...]
        pl.semaphore_wait(barrier, n - 1 + 1 + self.zs - 1)

        self.gather_start(0)
        self.spread(r.ng[0], 0)
        self.spread(r.gg[0], 1)
        self.tables()
        self.gather_mid(0)
        self.gather_start(1)
        self.gather_end(0)
        self.project(0, self.ha)
        for k in range(1, n):
            self.arrived(r.ng[0], 0, k)
            self.project(0, other(self.ha, k))
        self.attend(0, 0)
        r.middle[0][...] = x + self.collect(0)

        r.ng[1][mine] = normalize(r.middle[0][...], r.gains[1][...]).astype(BF16)
        self.spread(r.ng[1], 2)
        self.gather_mid(1)
        self.gather_start(2)
        self.gather_end(1)

        def ready_early():
            self.gather_mid(2)
            self.gather_start(3)
            self.gather_end(2)

        self.feed(0, 1, r.ng[1], 2, False, ready_early)
        r.between[...] = r.middle[0][...] + self.collect(1)

        r.ng[2][mine] = normalize(r.between[...], r.gains[2][...]).astype(BF16)
        self.spread(r.ng[2], 3)
        self.gather_mid(3)
        self.gather_start(4)
        self.gather_end(3)
        self.project(1, self.ha)
        for k in range(1, n):
            self.arrived(r.ng[2], 3, k)
            self.project(1, other(self.ha, k))
        self.attend(1, 2)
        self.gather_mid(4)
        self.gather_start(5)
        r.middle[1][...] = r.between[...] + self.collect(2)

        r.ng[3][mine] = normalize(r.middle[1][...], r.gains[3][...]).astype(BF16)
        self.spread(r.ng[3], 4)
        self.gather_end(4)
        for k in range(1, n):
            self.arrived(r.gg[0], 1, k)

        def ready_later():
            self.gather_mid(5)
            self.gather_end(5)

        self.feed(1, 3, r.ng[3], 4, True, ready_later)
        self.feed_grads(1)
        self.reduce_start(2)
        back, gain = norm_back(r.middle[1][...], r.gains[3][...], self.collect(3))
        r.gmid[...] = r.cot[...].astype(F32) + back
        r.gsum[3:4] = gain

        r.gg[1][mine] = r.gmid[...].astype(BF16)
        self.spread_done(r.gg[0], 1)
        self.spread(r.gg[1], 5)
        self.reduce_mid(2)
        self.pull(1, 5)
        for k in range(1, n):
            self.output_copy(k).start()
        self.attend_back(1, 4)
        self.attend_grads(1)
        self.reduce_start(3)
        self.reduce_merge(2)
        back, gain = norm_back(r.between[...], r.gains[2][...], self.collect(4))
        r.between[...] = r.gmid[...] + back
        r.gsum[2:3] = gain

        r.gg[0][mine] = r.between[...].astype(BF16)
        self.spread(r.gg[0], 6)
        self.reduce_mid(3)
        out = r.middle[1][...] + r.ypart[mine].astype(F32)
        for k in range(1, n):
            self.output_copy(k).wait_recv()
            out = out + r.yrecv[k].astype(F32)
        r.out[...] = out.astype(BF16)

        def back_block(where):
            return self.feed_back(0, where, 0, r.gate[where], r.up[where])[0]

        r.own[...] = back_block(mine)
        for k in range(1, n):
            self.arrived(r.gg[0], 6, k)
            where = rows_of(other(self.ha, k), self.rows)
            r.sbuf[k] = back_block(where).astype(BF16)
            self.part_copy(5, k, other(self.ha, k)).start()
        self.reduce_end(2)
        self.feed_grads(0)
        self.reduce_start(0)
        back, gain = norm_back(r.middle[0][...], r.gains[1][...], self.collect(5))
        r.gmid[...] = r.between[...] + back
        r.gsum[1:2] = gain

        self.spread_done(r.gg[1], 5)
        r.gg[1][mine] = r.gmid[...].astype(BF16)
        self.spread(r.gg[1], 7)
        self.reduce_mid(0)
        self.reduce_merge(3)
        self.pull(0, 7)
        self.attend_back(0, 6)
        self.reduce_end(3)
        self.attend_grads(0)
        self.reduce_start(1)
        self.reduce_merge(0)
        self.reduce_mid(1)
        back, gain = norm_back(x, r.gains[0][...], self.collect(6))
        r.gx[...] = r.gmid[...] + back
        r.gsum[0:1] = gain

        r.gbuf[0][self.ha] = r.gsum[...]
        self.gain_phase(0, "ha", self.ha, n, lambda t: t)
        self.reduce_end(0)
        r.gbuf[1][self.c] = self.gain_sum(0, "ha", self.ha, n, lambda t: t)
        self.gain_phase(1, "af", self.c, 2, lambda t: self.z * 2 + t)
        self.reduce_merge(1)
        r.gbuf[2][self.z] = self.gain_sum(1, "af", self.c, 2, lambda t: self.z * 2 + t)
        self.gain_phase(2, "af", self.z, self.zs, lambda t: t * 2 + self.c)
        total = self.gain_sum(2, "af", self.z, self.zs, lambda t: t * 2 + self.c)
        for i in range(4):
            r.gainsum[i] = total[i:i + 1]
        self.reduce_end(1)
        for slot, buffer in ((0, r.ng[0]), (2, r.ng[1]), (3, r.ng[2]), (4, r.ng[3]), (6, r.gg[0]), (7, r.gg[1])):
            self.spread_done(buffer, slot)
        for k in range(1, n):
            self.output_copy(k).wait_send()
        for i in range(6):
            self.gather_drain(i)

    def pull(self, layer, slot):
        r = self.r

        def block(where):
            r.gat[where] = mm(r.gg[1][where], self.matrix(3 * layer, 3)).astype(BF16)

        block(rows_of(self.ha, self.rows))
        for k in range(1, self.n):
            self.arrived(r.gg[1], slot, k)
            block(rows_of(other(self.ha, k), self.rows))


def step_kernel(n, g, names, *refs):
    found = {}
    for (name, index), ref in zip(names, refs):
        if index is None:
            found[name] = ref
        else:
            found.setdefault(name, {})[index] = ref
    Step(n, g, types.SimpleNamespace(**found)).run()


def finish_kernel(*refs):
    sums, gains, out, gx = refs[:4], refs[4], refs[5], refs[6]
    results, sem = refs[7:-1], refs[-1]
    pairs = [(out, results[0]), (gx, results[1])]
    for layer in range(2):
        first = 2 + 9 * layer
        pairs.append((gains.at[2 * layer], results[first]))
        pairs.append((gains.at[2 * layer + 1], results[first + 5]))
        pairs += [(sums[2 * layer + 1].at[j], results[first + 1 + j]) for j in range(4)]
        pairs += [(sums[2 * layer].at[j], results[first + 6 + j]) for j in range(3)]
    copies = [pltpu.make_async_copy(source, target, sem.at[k]) for k, (source, target) in enumerate(pairs)]
    for copy in copies:
        copy.start()
    for copy in copies:
        copy.wait()


def per_device(
    block_input, lengths, cotangent,
    attngain_early, query_early, keys_early, values_early, output_early,
    ffngain_early, gate_early, upward_early, down_early,
    attngain_later, query_later, keys_later, values_later, output_later,
    ffngain_later, gate_later, upward_later, down_later,
):
    n, g = lax.axis_size("ha"), lax.axis_size("af")
    zs = g // 2
    rows, depth = block_input.shape
    bucket = rows * n
    wrows, width = query_early.shape
    hidden = gate_early.shape[1]
    lane = np.arange(128)
    halfway = HD // 2
    frequency = np.float32(rope_base) ** (-(lane % halfway).astype(np.float32) / np.float32(halfway))
    wave = jnp.asarray(np.stack([frequency, np.where(lane % HD < halfway, -1.0, 1.0)]).astype(np.float32))
    flip = wrows % 128 == 0
    if flip:
        gate_early, upward_early, down_early = gate_early.T, upward_early.T, down_early.T
        gate_later, upward_later, down_later = gate_later.T, upward_later.T, down_later.T
    groups = [
        (query_early, keys_early, values_early, output_early), (gate_early, upward_early), (down_early,),
        (query_later, keys_later, values_later, output_later), (gate_later, upward_later), (down_later,),
    ]
    gains = [v[None, :] for v in (attngain_early, ffngain_early, attngain_later, ffngain_later)]

    names, args, in_specs = [], [], []

    def take(name, index, value, spec=VMEM):
        names.append((name, index))
        args.append(value)
        in_specs.append(spec)

    take("x", None, block_input)
    take("cot", None, cotangent)
    take("lengths", None, lengths, pl.BlockSpec(memory_space=pltpu.SMEM))
    take("wave", None, wave)
    for i, v in enumerate(gains):
        take("gains", i, v)
    for i, group in enumerate(groups):
        for j, v in enumerate(group):
            take("whbm", (i, j), v, ANY)

    outs = []

    def give(name, index, shape, kind):
        names.append((name, index))
        outs.append(jax.ShapeDtypeStruct(shape, kind))

    blocks = [(3, *down_early.shape), (4, wrows, width)] * 2
    for i, shape in enumerate(blocks):
        give("sums", i, shape, F32)
    give("gainsum", None, (4, 1, depth), F32)
    give("out", None, (rows, depth), BF16)
    give("gx", None, (rows, depth), F32)

    scratch = []

    def hold(name, index, shape, kind):
        names.append((name, index))
        scratch.append(pltpu.VMEM(shape, kind))

    for i, group in enumerate(groups):
        hold("w", i, (g, len(group), *group[0].shape), BF16)
    for i in range(4):
        hold("ng", i, (bucket, depth), BF16)
        hold("zrecv", i, (zs, *blocks[i]), BF16)
    for i in range(2):
        hold("part", i, (2, zs, *blocks[i]), BF16)
        hold("swapped", i, (zs, *blocks[i]), BF16)
        hold("gg", i, (bucket, depth), BF16)
        for name in ("q", "k", "v", "att"):
            hold(name, i, (bucket, width), BF16)
        hold("middle", i, (rows, depth), F32)
    for name in ("cos", "sin"):
        hold(name, None, (bucket, 128), F32)
    for name in ("first", "carry", "gva", "gka"):
        hold(name, None, (bucket, width), F32)
    for name in ("gat", "gq", "gk", "gv"):
        hold(name, None, (bucket, width), BF16)
    for name in ("gate", "up"):
        hold(name, None, (bucket, hidden), F32)
    for i in range(3):
        hold("units", i, (hidden, bucket) if flip else (bucket, hidden), BF16)
    for name in ("own", "between", "gmid"):
        hold(name, None, (rows, depth), F32)
    for name in ("sbuf", "rbuf", "yrecv"):
        hold(name, None, (n, rows, depth), BF16)
    hold("ypart", None, (bucket, depth), BF16)
    hold("gsum", None, (4, depth), F32)
    for i, count in enumerate((n, 2, zs)):
        hold("gbuf", i, (count, 4, depth), F32)
    for name, shape in (
        ("ags", (8, n)), ("agr", (8, n)), ("pss", (8, n)), ("psr", (8, n)), ("lsem", (6, 4)),
        ("gs", (6, 2, zs + 2)), ("gr", (6, 2, zs + 2)), ("rs", (4, zs + 3)), ("rr", (4, zs + 3)),
        ("gns", (3, max(n, zs))), ("gnr", (3, max(n, zs))),
    ):
        names.append((name, None))
        scratch.append(pltpu.SemaphoreType.DMA(shape))

    results = pl.pallas_call(
        functools.partial(step_kernel, n, g, names),
        out_shape=outs, in_specs=in_specs, out_specs=[VMEM] * len(outs), scratch_shapes=scratch,
        compiler_params=pltpu.CompilerParams(
            collective_id=0, has_side_effects=True, vmem_limit_bytes=63 * 1024 * 1024
        ),
        cost_estimate=pl.CostEstimate(flops=2 * 10**10, bytes_accessed=10**7, transcendentals=0),
        name="step",
    )(*args)

    shape = jax.ShapeDtypeStruct
    layer = (
        [shape((1, depth), F32)] + [shape((wrows, width), F32)] * 4
        + [shape((1, depth), F32)] + [shape(down_early.shape, F32)] * 3
    )
    finals = pl.pallas_call(
        finish_kernel,
        out_shape=[shape((rows, depth), BF16), shape((rows, depth), F32), *layer, *layer],
        in_specs=[ANY] * 7, out_specs=[VMEM] * 20, scratch_shapes=[pltpu.SemaphoreType.DMA((20,))], name="finish",
        compiler_params=pltpu.CompilerParams(vmem_limit_bytes=62 * 1024 * 1024),
    )(*results)
    finals = [v[0] if v.shape[0] == 1 else v for v in finals]
    if flip:
        finals = [v.T if v.shape == down_early.shape else v for v in finals]
    return tuple(finals)


def solution(mesh):
    tokens = P(("af", "ha"), None)
    matrix = P("af", "ha")
    layer = (P(), matrix, matrix, matrix, matrix, P(), matrix, matrix, matrix)
    return jax.shard_map(
        per_device, mesh=mesh,
        in_specs=(tokens, P("af", None), tokens, *layer, *layer),
        out_specs=(tokens, tokens, *layer, *layer),
        check_vma=False,
    )
```

```python
import functools
import types

import jax
import jax.numpy as jnp
import numpy as np
from jax import lax
from jax.experimental import pallas as pl
from jax.experimental.pallas import tpu as pltpu
from jax.sharding import PartitionSpec as P

HD = 64
epsilon = 1e-06
rope_base = 10000.0
MESH = pl.DeviceIdType.MESH
VMEM = pl.BlockSpec(memory_space=pltpu.VMEM)
ANY = pl.BlockSpec(memory_space=pl.ANY)
F32 = jnp.float32
BF16 = jnp.bfloat16


def mm(left, right):
    return jnp.dot(left, right, preferred_element_type=F32)


def mm_nt(left, right):
    return lax.dot_general(left, right, (((1,), (1,)), ((), ())), preferred_element_type=F32)


def mm_tn(left, right):
    return lax.dot_general(left, right, (((0,), (0,)), ((), ())), preferred_element_type=F32)


def normalize(values, gain):
    return values * lax.rsqrt(jnp.mean(values * values, axis=-1, keepdims=True) + epsilon) * gain


def norm_back(values, gain, grads):
    scaling = lax.rsqrt(jnp.mean(values * values, axis=-1, keepdims=True) + epsilon)
    weighted = gain * grads
    inner = jnp.mean(weighted * values, axis=-1, keepdims=True)
    return (
        scaling * weighted - values * scaling * scaling * scaling * inner,
        jnp.sum(grads * values * scaling, axis=0, keepdims=True),
    )


def other(me, k):
    result, bit = me, 1
    while bit <= k:
        if k & bit:
            result = result + bit * (1 - 2 * lax.rem(lax.div(me, bit), 2))
        bit *= 2
    return result


def swap_halves(values):
    width = values.shape[-1]
    lane = lax.broadcasted_iota(jnp.int32, values.shape, 1)
    half = HD // 2
    return jnp.where(
        lax.rem(lane, HD) < half,
        pltpu.roll(values, width - half, 1),
        pltpu.roll(values, half, 1),
    )


def head_masks(width, kind):
    lane = lax.broadcasted_iota(jnp.int32, (1, width), 1)
    return [(lax.div(lane, HD) == h).astype(kind) for h in range(width // HD)]


def stack_heads(block, masks):
    return jnp.concatenate([block * mask for mask in masks], axis=0)


def unstack_heads(stacked, masks, rows):
    total = None
    for h, mask in enumerate(masks):
        piece = stacked[h * rows:(h + 1) * rows] * mask
        total = piece if total is None else total + piece
    return total


def softmax_parts(scores, allowed, heads, rows):
    result = []
    for h in range(heads):
        masked = jnp.where(allowed, scores[h * rows:(h + 1) * rows] * (HD ** -0.5), -1000000000.0)
        weights = jnp.exp(masked - jnp.max(masked, axis=-1, keepdims=True))
        result.append(weights * (1.0 / jnp.sum(weights, axis=-1, keepdims=True)))
    return result


def rows_of(index, count):
    return pl.ds(pl.multiple_of(index * count, count), count)


def remote(source, target, send, recv, **place):
    return pltpu.make_async_remote_copy(
        src_ref=source, dst_ref=target, send_sem=send, recv_sem=recv, device_id=place, device_id_type=MESH
    )


class Step:
    def __init__(self, n, g, refs):
        self.n, self.g, self.zs = n, g, g // 2
        self.square = n == 4
        self.r = refs
        self.ha, self.af = lax.axis_index("ha"), lax.axis_index("af")
        self.z, self.c = lax.div(self.af, 2), lax.rem(self.af, 2)
        self.sibling = self.af + 1 - 2 * self.c
        self.rows, self.depth = refs.x.shape
        self.bucket = self.rows * n
        self.width = refs.q[0].shape[1]
        self.heads = self.width // HD
        self.hidden = refs.gate.shape[1]
        self.count = self.depth // g
        self.flip = refs.w[2].shape[3] == self.count
        self.ends = self.zs > 3
        self.reach = self.zs - 2 if self.ends else self.zs - 1


    def token_copy(self, buffer, slot, owner, k, target, half=None):
        rows = self.rows if half is None else self.rows // 2
        first = owner * self.rows if half is None else owner * self.rows + half * rows
        block = buffer.at[pl.ds(pl.multiple_of(first, rows), rows)]
        return remote(block, block, self.r.ags.at[slot, k], self.r.agr.at[slot, k], ha=target)

    def relay_copy(self, buffer, slot, k):
        return self.token_copy(buffer, slot, other(self.ha, k), 3 if k == 1 else 0, other(self.ha, 3 - k), k - 1)

    def spread(self, buffer, slot):
        for k in range(1, 3 if self.square else self.n):
            self.token_copy(buffer, slot, self.ha, k, other(self.ha, k)).start()

    def arrived(self, buffer, slot, k):
        if not self.square:
            self.token_copy(buffer, slot, other(self.ha, k), k, other(self.ha, k)).wait_recv()
        elif k == 1:
            for j in (1, 2):
                self.token_copy(buffer, slot, other(self.ha, j), j, other(self.ha, j)).wait_recv()
                self.relay_copy(buffer, slot, j).start()
        elif k == 3:
            for half in (0, 1):
                self.token_copy(
                    buffer, slot, other(self.ha, 3), 0 if half else 3, other(self.ha, 1 + half), half
                ).wait_recv()

    def spread_done(self, buffer, slot):
        for k in range(1, 3 if self.square else self.n):
            self.token_copy(buffer, slot, self.ha, k, other(self.ha, k)).wait_send()
        if self.square:
            for k in (1, 2):
                self.relay_copy(buffer, slot, k).wait_send()

    def part_copy(self, slot, k, target):
        return remote(self.r.sbuf.at[k], self.r.rbuf.at[k], self.r.pss.at[slot, k], self.r.psr.at[slot, k], ha=target)

    def ship(self, part, slot, index):
        for k in range(self.n):
            @pl.when(self.ha == (index ^ k))
            def _(k=k):
                if k == 0:
                    self.r.own[...] = part
                else:
                    self.r.sbuf[k] = part.astype(BF16)
                    self.part_copy(slot, k, index).start()

    def collect(self, slot):
        total = self.r.own[...]
        for k in range(1, self.n):
            self.part_copy(slot, k, other(self.ha, k)).wait_recv()
            total = total + self.r.rbuf[k].astype(F32)
        for k in range(1, self.n):
            self.part_copy(slot, k, other(self.ha, k)).wait_send()
        return total

    def output_copy(self, k):
        target = other(self.ha, k)
        return remote(
            self.r.ypart.at[rows_of(target, self.rows)], self.r.yrecv.at[k],
            self.r.pss.at[7, k], self.r.psr.at[7, k], ha=target,
        )


    def block(self, i, z, c):
        return self.r.w[i].at[z * 2 + c]

    def local_copy(self, i, j):
        return pltpu.make_async_copy(self.r.whbm[i, j], self.r.w[i].at[self.af, j], self.r.lsem.at[i, j])

    def to_sibling(self, i, z):
        block = self.block(i, z, self.c)
        return remote(block, block, self.r.gs.at[i, 0, z], self.r.gr.at[i, 0, z], af=self.sibling)

    def along(self, i, source, z, slot):
        block = self.block(i, source, self.c)
        return remote(block, block, self.r.gs.at[i, 1, slot], self.r.gr.at[i, 1, source], af=z * 2 + self.c)

    def neighbours(self, do, far_first=False):
        distances = range(1, self.reach + 1)
        for d in reversed(distances) if far_first else distances:
            for t in (self.z + d, self.z - d):
                pl.when((t >= 0) & (t < self.zs))(functools.partial(do, t))

    def onward(self, i, hop):
        result = []
        for side, sign in enumerate((1, -1)):
            source, target = self.z - sign * hop, self.z + sign
            valid = (source >= 0) & (source < self.zs) & (target >= 0) & (target < self.zs)
            result.append((valid, functools.partial(self.along, i, source, target, 2 * hop + side)))
        return result

    def gather_start(self, i):
        for j in range(self.r.w[i].shape[1]):
            self.local_copy(i, j).wait()
        for valid, copy in self.onward(i, 0):
            pl.when(valid)(lambda copy=copy: copy().start())
        self.to_sibling(i, self.z).start()

    def gather_hop(self, i, third):
        hops = self.zs - 1
        for hop in range((third - 1) * hops // 3 + 1, third * hops // 3 + 1):
            onward = self.onward(i, hop)
            for side, sign in enumerate((1, -1)):
                source = self.z - sign * hop

                def take(source=source, onward=onward[side]):
                    self.along(i, source, source, 0).wait_recv()
                    pl.when(onward[0])(lambda: onward[1]().start())
                    self.to_sibling(i, source).start()

                pl.when((source >= 0) & (source < self.zs))(take)

    def gather_end(self, i):
        for t in range(self.zs):
            block = self.block(i, t, 1 - self.c)
            remote(block, block, self.r.gs.at[i, 0, t], self.r.gr.at[i, 0, t], af=self.sibling).wait_recv()

    def gather_drain(self, i):
        for hop in range(self.zs - 1):
            for valid, copy in self.onward(i, hop):
                pl.when(valid)(lambda copy=copy: copy().wait_send())
        for t in range(self.zs):
            self.to_sibling(i, t).wait_send()


    def swap_copy(self, i):
        return remote(
            self.r.part[i % 4].at[1 - self.c], self.r.swapped[i % 4], self.r.rs.at[i, 0], self.r.rr.at[i, 0],
            af=self.sibling,
        )

    def sum_copy(self, i, source, z):
        return remote(
            self.r.part[i % 4].at[self.c, z], self.r.zrecv[i].at[source],
            self.r.rs.at[i, 1 + z], self.r.rr.at[i, 1 + source], af=z * 2 + self.c,
        )

    def merge_copy(self, i, up):
        last = self.zs - 1
        block, target = (last, 1) if up else (0, last - 1)
        slot = self.zs + (1 if up else 2)
        return remote(
            self.r.part[i % 4].at[self.c, block], self.r.zrecv[i].at[target],
            self.r.rs.at[i, slot], self.r.rr.at[i, slot], af=target * 2 + self.c,
        )

    def reduce_start(self, i):
        self.swap_copy(i).start()

    def reduce_mid(self, i):
        part, swapped, last = self.r.part[i % 4], self.r.swapped[i % 4], self.zs - 1
        self.swap_copy(i).wait_recv()

        def add(t, carry):
            part[self.c, t] = (part[self.c, t].astype(F32) + swapped[t].astype(F32)).astype(BF16)
            return carry

        lax.fori_loop(0, self.zs, add, 0)
        if self.ends:
            pl.when(self.z == 0)(lambda: self.merge_copy(i, True).start())
            pl.when(self.z == last)(lambda: self.merge_copy(i, False).start())

        def send(t):
            if self.ends:
                held = ((self.z == 1) & (t == last)) | ((self.z == last - 1) & (t == 0))
                pl.when(jnp.logical_not(held))(lambda: self.sum_copy(i, self.z, t).start())
            else:
                self.sum_copy(i, self.z, t).start()

        self.neighbours(send, far_first=True)

    def reduce_merge(self, i):
        part, last = self.r.part[i % 4], self.zs - 1
        if self.ends:
            def merge(up):
                block = last if up else 0
                self.merge_copy(i, up).wait_recv()
                part[self.c, block] = (
                    part[self.c, block].astype(F32) + self.r.zrecv[i][1 if up else last - 1].astype(F32)
                ).astype(BF16)
                self.sum_copy(i, self.z, block).start()

            pl.when(self.z == 1)(functools.partial(merge, True))
            pl.when(self.z == last - 1)(functools.partial(merge, False))

    def reduce_end(self, i):
        part, out, last = self.r.part[i % 4], self.r.sums[i], self.zs - 1
        out[...] = part[self.c, self.z].astype(F32)

        def take(t):
            self.sum_copy(i, t, t).wait_recv()
            out[...] += self.r.zrecv[i][t].astype(F32)

        self.neighbours(take)
        self.swap_copy(i).wait_send()
        self.neighbours(lambda t: self.sum_copy(i, self.z, t).wait_send())
        if self.ends:
            pl.when(self.z == 0)(lambda: self.merge_copy(i, True).wait_send())
            pl.when(self.z == last)(lambda: self.merge_copy(i, False).wait_send())

    def products(self, i, pairs):
        part, count = self.r.part[i % 4], self.count

        def chip(z, carry):
            here = pl.ds(pl.multiple_of(z * 2 * count, 2 * count), 2 * count)
            for j, left, right in pairs:
                if i % 4 >= 2 and self.flip:
                    product = mm(right[...], left[:, here]).astype(BF16)
                    part[0, z, j] = product[:, :count]
                    part[1, z, j] = product[:, count:]
                else:
                    product = mm_tn(left[:, here], right[...]).astype(BF16)
                    part[0, z, j] = product[:count]
                    part[1, z, j] = product[count:]
            return carry

        lax.fori_loop(0, self.zs, chip, 0)


    def tables(self):
        r = self.r
        count = r.lengths.shape[1]
        places = lax.broadcasted_iota(jnp.int32, (self.bucket, 1), 0)
        beginning = jnp.zeros((self.bucket, 1), jnp.int32)
        end = 0
        for s in range(count):
            start, end = end, end + r.lengths[0, s]
            beginning = jnp.where((places >= start) & (places < end), start, beginning)
        angles = (places - beginning).astype(F32) * r.wave[0:1]
        r.cos[...] = jnp.cos(angles)
        r.sin[...] = jnp.sin(angles) * r.wave[1:2]

    def turning(self, where):
        copies = self.width // 128
        return (
            jnp.concatenate([self.r.cos[where]] * copies, axis=1),
            jnp.concatenate([self.r.sin[where]] * copies, axis=1),
        )

    def allowed(self, i):
        span = (i + 1) * self.rows
        places_q = i * self.rows + lax.broadcasted_iota(jnp.int32, (self.rows, 1), 0)
        places_k = lax.broadcasted_iota(jnp.int32, (1, span), 1)
        qdoc = jnp.zeros((self.rows, 1), jnp.int32)
        kdoc = jnp.zeros((1, span), jnp.int32)
        end = 0
        for s in range(self.r.lengths.shape[1]):
            end = end + self.r.lengths[0, s]
            qdoc = qdoc + (places_q >= end).astype(jnp.int32)
            kdoc = kdoc + (places_k >= end).astype(jnp.int32)
        qdoc = jnp.where(places_q >= end, -1, qdoc)
        return ((qdoc == kdoc) & (places_k <= places_q)) | (places_k == places_q)

    def matrix(self, i, j):
        return self.r.w[i][:, j].reshape(self.depth, self.r.w[i].shape[-1])

    def turned(self, i, j):
        return jnp.concatenate([self.r.w[i][owner, j] for owner in range(self.g)], axis=1)

    def into_hidden(self, source, i, j):
        return mm_nt(source, self.turned(i, j)) if self.flip else mm(source, self.matrix(i, j))

    def out_of_hidden(self, source, i, j):
        return mm(source, self.turned(i, j)) if self.flip else mm_nt(source, self.matrix(i, j))


    def project(self, layer, block):
        r = self.r
        where = rows_of(block, self.rows)
        source = r.ng[2 * layer][where]
        cosine, sine = self.turning(where)
        raw = mm(source, self.matrix(4 * layer, 0))
        r.q[layer][where] = (raw * cosine + swap_halves(raw) * sine).astype(BF16)
        raw = mm(source, self.matrix(4 * layer, 1))
        r.k[layer][where] = (raw * cosine + swap_halves(raw) * sine).astype(BF16)
        raw = mm(source, self.matrix(4 * layer, 2))
        if layer == 0:
            r.first[where] = raw
            r.v[layer][where] = raw.astype(BF16)
        else:
            r.v[layer][where] = (0.5 * raw + 0.5 * r.first[where]).astype(BF16)

    def attend(self, layer, slot):
        r, rows = self.r, self.rows
        masks, masks32 = head_masks(self.width, BF16), head_masks(self.width, F32)
        for i in range(self.n):
            span = (i + 1) * rows
            here = slice(i * rows, span)
            scores = mm_nt(stack_heads(r.q[layer][here], masks), r.k[layer][:span])
            probs = [p.astype(BF16) for p in softmax_parts(scores, self.allowed(i), self.heads, rows)]
            mixed = mm(jnp.concatenate(probs, axis=0), r.v[layer][:span])
            block = unstack_heads(mixed, masks32, rows).astype(BF16)
            r.att[layer][here] = block
            self.ship(mm_nt(block, self.matrix(4 * layer + 1, 0)), slot, i)

    def attend_back(self, layer, slot):
        r, rows = self.r, self.rows
        masks, masks32 = head_masks(self.width, BF16), head_masks(self.width, F32)
        scale = HD ** -0.5
        for i in reversed(range(self.n)):
            span = (i + 1) * rows
            here = slice(i * rows, span)
            keys, vals = r.k[layer][:span], r.v[layer][:span]
            qs = stack_heads(r.q[layer][here], masks)
            gas = stack_heads(r.gat[here], masks)
            probs = softmax_parts(mm_nt(qs, keys), self.allowed(i), self.heads, rows)
            gprobs = mm_nt(gas, vals)
            raws = []
            for h in range(self.heads):
                p, gp = probs[h], gprobs[h * rows:(h + 1) * rows]
                inner = jnp.sum(p * gp, axis=-1, keepdims=True)
                raws.append((p * (gp - inner) * scale).astype(BF16))
            raw = jnp.concatenate(raws, axis=0)
            low = jnp.concatenate([p.astype(BF16) for p in probs], axis=0)
            if i == self.n - 1:
                r.gva[...] = mm_tn(low, gas)
                r.gka[...] = mm_tn(raw, qs)
            else:
                r.gva[:span] += mm_tn(low, gas)
                r.gka[:span] += mm_tn(raw, qs)
            cosine, sine = self.turning(here)
            gqr = unstack_heads(mm(raw, keys), masks32, rows)
            gqr = (gqr * cosine - swap_halves(gqr) * sine).astype(BF16)
            gkr = r.gka[here]
            gkr = (gkr * cosine - swap_halves(gkr) * sine).astype(BF16)
            if layer == 1:
                half = 0.5 * r.gva[here]
                r.carry[here] = half
                gvr = half.astype(BF16)
            else:
                gvr = (r.gva[here] + r.carry[here]).astype(BF16)
            r.gq[here], r.gk[here], r.gv[here] = gqr, gkr, gvr
            part = (
                mm_nt(gqr, self.matrix(4 * layer, 0))
                + mm_nt(gkr, self.matrix(4 * layer, 1))
                + mm_nt(gvr, self.matrix(4 * layer, 2))
            )
            self.ship(part, slot, i)

    def feed(self, slot, buffer, agslot, ready):
        r = self.r

        def first(where):
            source = buffer[where]
            r.gate[where] = self.into_hidden(source, 2, 0)
            r.up[where] = self.into_hidden(source, 2, 1)

        def second(where):
            g, u = r.gate[where], r.up[where]
            return self.out_of_hidden((g * jax.nn.sigmoid(g) * u).astype(BF16), 3, 0)

        places = [rows_of(other(self.ha, k), self.rows) for k in range(self.n)]
        first(places[0])
        for k in range(1, self.n):
            if k == self.n - 1:
                ready()
                r.own[...] = second(places[0])
                for j in range(1, k):
                    self.send_part(slot, j, second(places[j]))
            self.arrived(buffer, agslot, k)
            first(places[k])
        self.send_part(slot, self.n - 1, second(places[self.n - 1]))

    def feed_turn(self, slot, buffer, agslot):
        r = self.r
        for k in range(self.n):
            if k > 0:
                self.arrived(buffer, agslot, k)
            where = rows_of(other(self.ha, k), self.rows)
            source = buffer[where]
            g, u = self.into_hidden(source, 6, 0), self.into_hidden(source, 6, 1)
            part, h = self.feed_back(1, where, 0, g, u)
            if k == 0:
                r.own[...] = part
            else:
                self.send_part(slot, k, part)
            r.ypart[where] = self.out_of_hidden(h, 7, 0).astype(BF16)

    def send_part(self, slot, k, part):
        self.r.sbuf[k] = part.astype(BF16)
        self.part_copy(slot, k, other(self.ha, k)).start()

    def feed_back(self, layer, where, gg, g, u):
        r = self.r
        s = jax.nn.sigmoid(g)
        h = (g * s * u).astype(BF16)
        gh = self.into_hidden(r.gg[gg][where], 4 * layer + 3, 0)
        a = (gh * u * s * (1.0 + g * (1.0 - s))).astype(BF16)
        b = (gh * g * s).astype(BF16)
        for j, value in enumerate((a, b, h)):
            if self.flip:
                r.units[j][:, where] = value.T
            else:
                r.units[j][where] = value
        return self.out_of_hidden(a, 4 * layer + 2, 0) + self.out_of_hidden(b, 4 * layer + 2, 1), h

    def down_grads(self, layer):
        self.products(4 * layer + 3, [(0, self.r.gg[0], self.r.units[2])])
        self.reduce_start(4 * layer + 3)

    def gate_grads(self, layer):
        normed = self.r.ng[2 * layer + 1]
        self.products(4 * layer + 2, [(0, normed, self.r.units[0]), (1, normed, self.r.units[1])])
        self.reduce_start(4 * layer + 2)

    def output_grads(self, layer):
        self.products(4 * layer + 1, [(0, self.r.gg[1], self.r.att[layer])])
        self.reduce_start(4 * layer + 1)

    def head_grads(self, layer):
        r = self.r
        normed = r.ng[2 * layer]
        self.products(4 * layer, [(0, normed, r.gq), (1, normed, r.gk), (2, normed, r.gv)])
        self.reduce_start(4 * layer)


    def gain_phase(self, slot, axis, me, count, place):
        buffer = self.r.gbuf[slot]
        for t in range(count):
            copy = remote(
                buffer.at[me], buffer.at[me], self.r.gns.at[slot, t], self.r.gnr.at[slot, me], **{axis: place(t)}
            )
            pl.when(me != t)(copy.start)

    def gain_sum(self, slot, axis, me, count, place):
        buffer = self.r.gbuf[slot]
        for t in range(count):
            copy = remote(
                buffer.at[t], buffer.at[t], self.r.gns.at[slot, t], self.r.gnr.at[slot, t], **{axis: place(t)}
            )
            pl.when(me != t)(copy.wait)
        total = buffer[0]
        for t in range(1, count):
            total = total + buffer[t]
        return total

    def run(self):
        r, n = self.r, self.n
        barrier = pltpu.get_barrier_semaphore()
        for k in range(1, n):
            pl.semaphore_signal(barrier, inc=1, device_id={"ha": other(self.ha, k)}, device_id_type=MESH)
        pl.semaphore_signal(barrier, inc=1, device_id={"af": self.sibling}, device_id_type=MESH)
        for d in range(1, self.zs):
            t = lax.rem(self.z + d, self.zs)
            pl.semaphore_signal(barrier, inc=1, device_id={"af": t * 2 + self.c}, device_id_type=MESH)
        for i in range(8):
            for j in range(r.w[i].shape[1]):
                self.local_copy(i, j).start()
        mine = rows_of(self.ha, self.rows)
        x = r.x[...].astype(F32)
        r.ng[0][mine] = normalize(x, r.gains[0][...]).astype(BF16)
        r.gg[0][mine] = r.cot[...]
        pl.semaphore_wait(barrier, n - 1 + 1 + self.zs - 1)

        self.gather_start(0)
        self.gather_start(1)
        self.spread(r.ng[0], 0)
        self.tables()
        self.gather_hop(0, 1)
        self.gather_start(2)
        self.arrived(r.ng[0], 0, 1)
        self.gather_hop(1, 1)
        self.gather_hop(0, 2)
        for k in range(2, n):
            self.arrived(r.ng[0], 0, k)
        self.spread(r.gg[0], 1)
        self.gather_hop(1, 2)
        self.gather_hop(0, 3)
        self.gather_end(0)
        for k in range(n):
            self.project(0, other(self.ha, k))
        self.gather_hop(1, 3)
        self.gather_end(1)
        self.gather_hop(2, 1)
        self.gather_start(3)
        self.attend(0, 0)
        self.arrived(r.gg[0], 1, 1)
        self.gather_hop(2, 2)
        r.middle[0][...] = x + self.collect(0)

        r.ng[1][mine] = normalize(r.middle[0][...], r.gains[1][...]).astype(BF16)
        self.spread(r.ng[1], 2)
        self.gather_hop(3, 1)
        self.gather_start(4)
        self.gather_start(5)
        self.gather_hop(2, 3)
        self.gather_end(2)
        self.gather_hop(3, 2)

        def ready():
            self.gather_hop(3, 3)
            self.gather_start(6)
            self.gather_end(3)

        self.feed(1, r.ng[1], 2, ready)
        for third in (1, 2):
            self.gather_hop(4, third)
            self.gather_hop(5, third)
        r.between[...] = r.middle[0][...] + self.collect(1)

        r.ng[2][mine] = normalize(r.between[...], r.gains[2][...]).astype(BF16)
        self.spread(r.ng[2], 3)
        self.gather_hop(4, 3)
        self.gather_hop(5, 3)
        self.gather_start(7)
        self.gather_end(4)
        self.project(1, self.ha)
        self.gather_hop(6, 1)
        for k in range(1, n):
            self.arrived(r.ng[2], 3, k)
            self.project(1, other(self.ha, k))
        self.gather_end(5)
        self.gather_hop(6, 2)
        self.attend(1, 2)
        self.gather_hop(7, 1)
        self.gather_hop(6, 3)
        r.middle[1][...] = r.between[...] + self.collect(2)

        r.ng[3][mine] = normalize(r.middle[1][...], r.gains[3][...]).astype(BF16)
        self.spread(r.ng[3], 4)
        self.gather_hop(7, 2)
        self.gather_end(6)
        for k in range(2, n):
            self.arrived(r.gg[0], 1, k)
        self.gather_hop(7, 3)
        self.gather_end(7)
        self.feed_turn(3, r.ng[3], 4)
        self.down_grads(1)
        self.gate_grads(1)
        self.reduce_mid(7)
        back, gain = norm_back(r.middle[1][...], r.gains[3][...], self.collect(3))
        r.gmid[...] = r.cot[...].astype(F32) + back
        r.gsum[3:4] = gain

        r.gg[1][mine] = r.gmid[...].astype(BF16)
        self.spread_done(r.gg[0], 1)
        self.spread(r.gg[1], 5)
        self.reduce_mid(6)
        self.pull(1, 5)
        for k in range(1, n):
            self.output_copy(k).start()
        self.output_grads(1)
        self.attend_back(1, 4)
        self.reduce_merge(7)
        self.head_grads(1)
        self.reduce_mid(5)
        self.reduce_merge(6)
        back, gain = norm_back(r.between[...], r.gains[2][...], self.collect(4))
        r.between[...] = r.gmid[...] + back
        r.gsum[2:3] = gain

        r.gg[0][mine] = r.between[...].astype(BF16)
        self.spread_done(r.gg[1], 5)
        self.spread(r.gg[0], 6)
        self.reduce_mid(4)
        out = r.middle[1][...] + r.ypart[mine].astype(F32)
        for k in range(1, n):
            self.output_copy(k).wait_recv()
            out = out + r.yrecv[k].astype(F32)
        r.out[...] = out.astype(BF16)
        self.reduce_merge(5)
        self.reduce_end(7)

        def back_block(where):
            return self.feed_back(0, where, 0, r.gate[where], r.up[where])[0]

        r.own[...] = back_block(mine)
        for k in range(1, n):
            self.arrived(r.gg[0], 6, k)
            self.send_part(5, k, back_block(rows_of(other(self.ha, k), self.rows)))
        self.down_grads(0)
        self.reduce_end(6)
        self.gate_grads(0)
        self.reduce_mid(3)
        self.reduce_merge(4)
        back, gain = norm_back(r.middle[0][...], r.gains[1][...], self.collect(5))
        r.gmid[...] = r.between[...] + back
        r.gsum[1:2] = gain

        r.gg[1][mine] = r.gmid[...].astype(BF16)
        self.spread(r.gg[1], 7)
        self.reduce_mid(2)
        self.reduce_end(5)
        self.pull(0, 7)
        self.output_grads(0)
        self.attend_back(0, 6)
        self.reduce_merge(3)
        self.reduce_end(4)
        self.head_grads(0)
        self.reduce_mid(1)
        self.reduce_merge(2)
        self.reduce_mid(0)
        back, gain = norm_back(x, r.gains[0][...], self.collect(6))
        r.gx[...] = r.gmid[...] + back
        r.gsum[0:1] = gain

        r.gbuf[0][self.ha] = r.gsum[...]
        self.gain_phase(0, "ha", self.ha, n, lambda t: t)
        self.reduce_merge(1)
        self.reduce_end(3)
        r.gbuf[1][self.c] = self.gain_sum(0, "ha", self.ha, n, lambda t: t)
        self.gain_phase(1, "af", self.c, 2, lambda t: self.z * 2 + t)
        self.reduce_merge(0)
        r.gbuf[2][self.z] = self.gain_sum(1, "af", self.c, 2, lambda t: self.z * 2 + t)
        self.gain_phase(2, "af", self.z, self.zs, lambda t: t * 2 + self.c)
        self.reduce_end(2)
        total = self.gain_sum(2, "af", self.z, self.zs, lambda t: t * 2 + self.c)
        for i in range(4):
            r.gainsum[i] = total[i:i + 1]
        self.reduce_end(1)
        self.reduce_end(0)
        for slot, buffer in ((0, r.ng[0]), (2, r.ng[1]), (3, r.ng[2]), (4, r.ng[3]), (6, r.gg[0]), (7, r.gg[1])):
            self.spread_done(buffer, slot)
        for k in range(1, n):
            self.output_copy(k).wait_send()
        for i in range(8):
            self.gather_drain(i)

    def pull(self, layer, slot):
        r = self.r

        def block(where):
            r.gat[where] = mm(r.gg[1][where], self.matrix(4 * layer + 1, 0)).astype(BF16)

        block(rows_of(self.ha, self.rows))
        for k in range(1, self.n):
            self.arrived(r.gg[1], slot, k)
            block(rows_of(other(self.ha, k), self.rows))


def step_kernel(n, g, names, *refs):
    found = {}
    for (name, index), ref in zip(names, refs):
        if index is None:
            found[name] = ref
        else:
            found.setdefault(name, {})[index] = ref
    Step(n, g, types.SimpleNamespace(**found)).run()


def finish_kernel(*refs):
    sums, gains, out, gx = refs[:8], refs[8], refs[9], refs[10]
    results, held, sem = refs[11:31], refs[31:-1], refs[-1]
    pairs = [(out, 0), (gx, 1)]
    for layer in range(2):
        first = 2 + 9 * layer
        pairs += [(gains.at[2 * layer], first), (gains.at[2 * layer + 1], first + 5)]
        pairs += [(sums[4 * layer].at[j], first + 1 + j) for j in range(3)]
        pairs.append((sums[4 * layer + 1].at[0], first + 4))
        pairs += [(sums[4 * layer + 2].at[j], first + 6 + j) for j in range(2)]
        pairs.append((sums[4 * layer + 3].at[0], first + 8))
    into = [pltpu.make_async_copy(source, held[k], sem.at[0, k]) for source, k in pairs]
    onward = [pltpu.make_async_copy(held[k], results[k], sem.at[1, k]) for _, k in pairs]
    for copy in into:
        copy.start()
    for first, second in zip(into, onward):
        first.wait()
        second.start()
    for copy in onward:
        copy.wait()


def per_device(
    block_input, lengths, cotangent,
    attngain_early, query_early, keys_early, values_early, output_early,
    ffngain_early, gate_early, upward_early, down_early,
    attngain_later, query_later, keys_later, values_later, output_later,
    ffngain_later, gate_later, upward_later, down_later,
):
    n, g = lax.axis_size("ha"), lax.axis_size("af")
    zs = g // 2
    rows, depth = block_input.shape
    bucket = rows * n
    wrows, width = query_early.shape
    hidden = gate_early.shape[1]
    lane = np.arange(128)
    halfway = HD // 2
    frequency = np.float32(rope_base) ** (-(lane % halfway).astype(np.float32) / np.float32(halfway))
    wave = jnp.asarray(np.stack([frequency, np.where(lane % HD < halfway, -1.0, 1.0)]).astype(np.float32))
    flip = wrows % 128 == 0
    if flip:
        gate_early, upward_early, down_early = gate_early.T, upward_early.T, down_early.T
        gate_later, upward_later, down_later = gate_later.T, upward_later.T, down_later.T
    groups = [
        (query_early, keys_early, values_early), (output_early,), (gate_early, upward_early), (down_early,),
        (query_later, keys_later, values_later), (output_later,), (gate_later, upward_later), (down_later,),
    ]
    gains = [v[None, :] for v in (attngain_early, ffngain_early, attngain_later, ffngain_later)]

    names, args, in_specs = [], [], []

    def take(name, index, value, spec=VMEM):
        names.append((name, index))
        args.append(value)
        in_specs.append(spec)

    take("x", None, block_input)
    take("cot", None, cotangent)
    take("lengths", None, lengths, pl.BlockSpec(memory_space=pltpu.SMEM))
    take("wave", None, wave)
    for i, v in enumerate(gains):
        take("gains", i, v)
    for i, group in enumerate(groups):
        for j, v in enumerate(group):
            take("whbm", (i, j), v, ANY)

    outs = []

    def give(name, index, shape, kind):
        names.append((name, index))
        outs.append(jax.ShapeDtypeStruct(shape, kind))

    blocks = [(len(group), *group[0].shape) for group in groups]
    for i, shape in enumerate(blocks):
        give("sums", i, shape, F32)
    give("gainsum", None, (4, 1, depth), F32)
    give("out", None, (rows, depth), BF16)
    give("gx", None, (rows, depth), F32)

    scratch = []

    def hold(name, index, shape, kind):
        names.append((name, index))
        scratch.append(pltpu.VMEM(shape, kind))

    for i, group in enumerate(groups):
        hold("w", i, (g, len(group), *group[0].shape), BF16)
    for i in range(8):
        hold("zrecv", i, (zs, *blocks[i]), BF16)
    for i in range(4):
        hold("ng", i, (bucket, depth), BF16)
        hold("part", i, (2, zs, *blocks[i]), BF16)
        hold("swapped", i, (zs, *blocks[i]), BF16)
    for i in range(2):
        hold("gg", i, (bucket, depth), BF16)
        for name in ("q", "k", "v", "att"):
            hold(name, i, (bucket, width), BF16)
        hold("middle", i, (rows, depth), F32)
    for name in ("cos", "sin"):
        hold(name, None, (bucket, 128), F32)
    for name in ("first", "carry", "gva", "gka"):
        hold(name, None, (bucket, width), F32)
    for name in ("gat", "gq", "gk", "gv"):
        hold(name, None, (bucket, width), BF16)
    for name in ("gate", "up"):
        hold(name, None, (bucket, hidden), F32)
    for i in range(3):
        hold("units", i, (hidden, bucket) if flip else (bucket, hidden), BF16)
    for name in ("own", "between", "gmid"):
        hold(name, None, (rows, depth), F32)
    for name in ("sbuf", "rbuf", "yrecv"):
        hold(name, None, (n, rows, depth), BF16)
    hold("ypart", None, (bucket, depth), BF16)
    hold("gsum", None, (4, depth), F32)
    for i, count in enumerate((n, 2, zs)):
        hold("gbuf", i, (count, 4, depth), F32)
    for name, shape in (
        ("ags", (8, n)), ("agr", (8, n)), ("pss", (8, n)), ("psr", (8, n)), ("lsem", (8, 3)),
        ("gs", (8, 2, 2 * zs)), ("gr", (8, 2, zs)), ("rs", (8, zs + 3)), ("rr", (8, zs + 3)),
        ("gns", (3, max(n, zs))), ("gnr", (3, max(n, zs))),
    ):
        names.append((name, None))
        scratch.append(pltpu.SemaphoreType.DMA(shape))

    results = pl.pallas_call(
        functools.partial(step_kernel, n, g, names),
        out_shape=outs, in_specs=in_specs, out_specs=[VMEM] * len(outs), scratch_shapes=scratch,
        compiler_params=pltpu.CompilerParams(
            collective_id=0, has_side_effects=True, vmem_limit_bytes=63 * 1024 * 1024
        ),
        cost_estimate=pl.CostEstimate(flops=2 * 10**10, bytes_accessed=10**7, transcendentals=0),
        name="step",
    )(*args)

    shape = jax.ShapeDtypeStruct
    layer = (
        [shape((1, depth), F32)] + [shape((wrows, width), F32)] * 4
        + [shape((1, depth), F32)] + [shape(down_early.shape, F32)] * 3
    )
    final_shapes = [shape((rows, depth), BF16), shape((rows, depth), F32), *layer, *layer]
    finals = pl.pallas_call(
        finish_kernel,
        out_shape=final_shapes, in_specs=[ANY] * 11, out_specs=[ANY] * 20,
        scratch_shapes=[*(pltpu.VMEM(v.shape, v.dtype) for v in final_shapes), pltpu.SemaphoreType.DMA((2, 20))],
        compiler_params=pltpu.CompilerParams(vmem_limit_bytes=62 * 1024 * 1024), name="finish",
    )(*results)
    finals = [v[0] if v.shape[0] == 1 else v for v in finals]
    if flip:
        finals = [v.T if v.shape == down_early.shape else v for v in finals]
    return tuple(finals)


def solution(mesh):
    tokens = P(("af", "ha"), None)
    matrix = P("af", "ha")
    layer = (P(), matrix, matrix, matrix, matrix, P(), matrix, matrix, matrix)
    return jax.shard_map(
        per_device, mesh=mesh,
        in_specs=(tokens, P("af", None), tokens, *layer, *layer),
        out_specs=(tokens, tokens, *layer, *layer),
        check_vma=False,
    )
```

```python
import functools
import types

import jax
import jax.numpy as jnp
import numpy as np
from jax import lax
from jax.experimental import pallas as pl
from jax.experimental.pallas import tpu as pltpu
from jax.sharding import PartitionSpec as P

HD = 64
CHUNKS = 1
epsilon = 1e-06
rope_base = 10000.0
MESH = pl.DeviceIdType.MESH
VMEM = pl.BlockSpec(memory_space=pltpu.VMEM)
ANY = pl.BlockSpec(memory_space=pl.ANY)
F32 = jnp.float32
BF16 = jnp.bfloat16


def mm(left, right):
    return jnp.dot(left, right, preferred_element_type=F32)


def mm_nt(left, right):
    return lax.dot_general(left, right, (((1,), (1,)), ((), ())), preferred_element_type=F32)


def mm_tn(left, right):
    return lax.dot_general(left, right, (((0,), (0,)), ((), ())), preferred_element_type=F32)


def normalize(values, gain):
    return values * lax.rsqrt(jnp.mean(values * values, axis=-1, keepdims=True) + epsilon) * gain


def norm_back(values, gain, grads):
    scaling = lax.rsqrt(jnp.mean(values * values, axis=-1, keepdims=True) + epsilon)
    weighted = gain * grads
    inner = jnp.mean(weighted * values, axis=-1, keepdims=True)
    return (
        scaling * weighted - values * scaling * scaling * scaling * inner,
        jnp.sum(grads * values * scaling, axis=0, keepdims=True),
    )


def other(me, k):
    result, bit = me, 1
    while bit <= k:
        if k & bit:
            result = result + bit * (1 - 2 * lax.rem(lax.div(me, bit), 2))
        bit *= 2
    return result


def swap_halves(values):
    width = values.shape[-1]
    lane = lax.broadcasted_iota(jnp.int32, values.shape, 1)
    half = HD // 2
    return jnp.where(
        lax.rem(lane, HD) < half,
        pltpu.roll(values, width - half, 1),
        pltpu.roll(values, half, 1),
    )


def head_masks(width, kind):
    lane = lax.broadcasted_iota(jnp.int32, (1, width), 1)
    return [(lax.div(lane, HD) == h).astype(kind) for h in range(width // HD)]


def stack_heads(block, masks):
    return jnp.concatenate([block * mask for mask in masks], axis=0)


def unstack_heads(stacked, masks, rows):
    total = None
    for h, mask in enumerate(masks):
        piece = stacked[h * rows:(h + 1) * rows] * mask
        total = piece if total is None else total + piece
    return total


def softmax_parts(scores, allowed, heads, rows):
    result = []
    for h in range(heads):
        masked = jnp.where(allowed, scores[h * rows:(h + 1) * rows] * (HD ** -0.5), -1000000000.0)
        weights = jnp.exp(masked - jnp.max(masked, axis=-1, keepdims=True))
        result.append(weights * (1.0 / jnp.sum(weights, axis=-1, keepdims=True)))
    return result


def rows_of(index, count):
    return pl.ds(pl.multiple_of(index * count, count), count)


def remote(source, target, send, recv, **place):
    return pltpu.make_async_remote_copy(
        src_ref=source, dst_ref=target, send_sem=send, recv_sem=recv, device_id=place, device_id_type=MESH
    )


class Step:
    def __init__(self, n, g, refs):
        self.n, self.g, self.zs = n, g, g // 2
        self.square = n == 4
        self.chunks = refs.agr.shape[2]
        self.r = refs
        self.ha, self.af = lax.axis_index("ha"), lax.axis_index("af")
        self.z, self.c = lax.div(self.af, 2), lax.rem(self.af, 2)
        self.sibling = self.af + 1 - 2 * self.c
        self.rows, self.depth = refs.x.shape
        self.bucket = self.rows * n
        self.step = self.rows // self.chunks
        if self.square:
            self.near, self.far = [(c, (1, 2)) for c in range(self.chunks)], [(c, (3,)) for c in range(self.chunks)]
            self.order = self.near[:1]
            for c in range(1, self.chunks):
                self.order += [self.near[c], self.far[c - 1]]
            self.order.append(self.far[-1])
        else:
            self.near, self.far = [(c, (k,)) for c in range(self.chunks) for k in range(1, n)], []
            self.order = self.near
        self.width = refs.q[0].shape[1]
        self.heads = self.width // HD
        self.hidden = refs.gate.shape[1]
        self.count = self.depth // g
        self.flip = refs.w[2].shape[3] == self.count


    def chunk(self, c):
        return slice(c * self.step, (c + 1) * self.step)

    def chunk_of(self, owner, c):
        return pl.ds(pl.multiple_of(owner * self.rows + c * self.step, self.step), self.step)

    def token_copy(self, buffer, slot, owner, c, k, target, half=None):
        count = self.step if half is None else self.step // 2
        first = owner * self.rows + c * self.step + (0 if half is None else half * count)
        block = buffer.at[pl.ds(pl.multiple_of(first, count), count)]
        return remote(block, block, self.r.ags.at[slot, k, c], self.r.agr.at[slot, k, c], ha=target)

    def relay_copy(self, buffer, slot, c, k):
        return self.token_copy(buffer, slot, other(self.ha, k), c, 3 if k == 1 else 0, other(self.ha, 3 - k), k - 1)

    def spread(self, buffer, slot, c):
        for k in range(1, 3 if self.square else self.n):
            self.token_copy(buffer, slot, self.ha, c, k, other(self.ha, k)).start()

    def spread_all(self, buffer, slot):
        for c in range(self.chunks):
            self.spread(buffer, slot, c)

    def arrived(self, buffer, slot, places):
        for c, ks in places:
            for k in ks:
                partner = other(self.ha, k)
                if self.square and k == 3:
                    for half in (0, 1):
                        self.token_copy(
                            buffer, slot, partner, c, 0 if half else 3, other(self.ha, 1 + half), half
                        ).wait_recv()
                else:
                    self.token_copy(buffer, slot, partner, c, k, partner).wait_recv()
                    if self.square:
                        self.relay_copy(buffer, slot, c, k).start()

    def spread_done(self, buffer, slot):
        for c in range(self.chunks):
            for k in range(1, 3 if self.square else self.n):
                self.token_copy(buffer, slot, self.ha, c, k, other(self.ha, k)).wait_send()
            if self.square:
                for k in (1, 2):
                    self.relay_copy(buffer, slot, c, k).wait_send()

    def each_block(self, buffer, slot, do):
        do(self.ha)
        for places in (self.near, self.far):
            self.arrived(buffer, slot, places)
            for k in sorted({k for _, ks in places for k in ks}):
                do(other(self.ha, k))

    def part_copy(self, slot, k, c, target):
        here = self.chunk(c)
        return remote(
            self.r.sbuf.at[k, here], self.r.rbuf.at[k, here], self.r.pss.at[slot, k, c], self.r.psr.at[slot, k, c],
            ha=target,
        )

    def ship(self, part, slot, index):
        for k in range(self.n):
            @pl.when(self.ha == (index ^ k))
            def _(k=k):
                if k == 0:
                    self.r.own[...] = part
                else:
                    self.r.sbuf[k] = part.astype(BF16)
                    for c in range(self.chunks):
                        self.part_copy(slot, k, c, index).start()

    def send_parts(self, slot, c, ks, part):
        for j, k in enumerate(ks):
            self.r.sbuf[k, self.chunk(c)] = part[self.chunk(j)].astype(BF16)
            self.part_copy(slot, k, c, other(self.ha, k)).start()

    def collect(self, slot, c):
        here = self.chunk(c)
        total = self.r.own[here]
        for k in range(1, self.n):
            self.part_copy(slot, k, c, other(self.ha, k)).wait_recv()
            total = total + self.r.rbuf[k, here].astype(F32)
        return total

    def parts_done(self, slot):
        for c in range(self.chunks):
            for k in range(1, self.n):
                self.part_copy(slot, k, c, other(self.ha, k)).wait_send()

    def output_copy(self, k):
        target = other(self.ha, k)
        return remote(
            self.r.ypart.at[rows_of(target, self.rows)], self.r.yrecv.at[k],
            self.r.pss.at[7, k, 0], self.r.psr.at[7, k, 0], ha=target,
        )


    def block(self, i, z, c):
        return self.r.w[i].at[z * 2 + c]

    def local_copy(self, i, j):
        return pltpu.make_async_copy(self.r.whbm[i, j], self.r.w[i].at[self.af, j], self.r.lsem.at[i, j])

    def to_sibling(self, i, z):
        block = self.block(i, z, self.c)
        return remote(block, block, self.r.gs.at[i, 0, z], self.r.gr.at[i, 0, z], af=self.sibling)

    def along(self, i, source, z, slot):
        block = self.block(i, source, self.c)
        return remote(block, block, self.r.gs.at[i, 1, slot], self.r.gr.at[i, 1, source], af=z * 2 + self.c)

    def onward(self, i, hop):
        result = []
        for side, sign in enumerate((1, -1)):
            source, target = self.z - sign * hop, self.z + sign
            valid = (source >= 0) & (source < self.zs) & (target >= 0) & (target < self.zs)
            result.append((valid, functools.partial(self.along, i, source, target, 2 * hop + side)))
        return result

    def gather_start(self, i):
        for j in range(self.r.w[i].shape[1]):
            self.local_copy(i, j).wait()
        for valid, copy in self.onward(i, 0):
            pl.when(valid)(lambda copy=copy: copy().start())
        self.to_sibling(i, self.z).start()

    def gather_hop(self, i, third):
        hops = self.zs - 1
        for hop in range((third - 1) * hops // 3 + 1, third * hops // 3 + 1):
            onward = self.onward(i, hop)
            for side, sign in enumerate((1, -1)):
                source = self.z - sign * hop

                def take(source=source, onward=onward[side]):
                    self.along(i, source, source, 0).wait_recv()
                    pl.when(onward[0])(lambda: onward[1]().start())
                    self.to_sibling(i, source).start()

                pl.when((source >= 0) & (source < self.zs))(take)

    def gather_end(self, i):
        for t in range(self.zs):
            block = self.block(i, t, 1 - self.c)
            remote(block, block, self.r.gs.at[i, 0, t], self.r.gr.at[i, 0, t], af=self.sibling).wait_recv()

    def gather_drain(self, i):
        for hop in range(self.zs - 1):
            for valid, copy in self.onward(i, hop):
                pl.when(valid)(lambda copy=copy: copy().wait_send())
        for t in range(self.zs):
            self.to_sibling(i, t).wait_send()


    def swap_copy(self, i):
        return remote(
            self.r.part[i % 4].at[1 - self.c], self.r.swapped[i % 4], self.r.rs.at[i, 0], self.r.rr.at[i, 0],
            af=self.sibling,
        )

    def flow(self, i, stage, side):
        last = self.zs - 1
        target = self.z + (1 if side == 0 else -1)
        upper = lax.div(2 * target, self.zs)
        if side == 0:
            valid = (target <= last) & (target <= stage)
            block = last - stage + target
            slot = block if stage < last else target * (1 - upper)
        else:
            valid = (target >= 0) & (last - target <= stage)
            block = stage - last + target
            slot = block if stage < last else target + (last - target) * (1 - upper)
        sem = 2 * stage + side
        return valid, functools.partial(
            remote, self.r.part[i % 4].at[self.c, block], self.r.zrecv[i].at[slot],
            self.r.rs.at[i, sem], self.r.rr.at[i, sem], af=target * 2 + self.c,
        )

    def taken(self, i, stage, side, use):
        last = self.zs - 1
        upper = lax.div(2 * self.z, self.zs)
        if side == 0:
            valid = (self.z >= 1) & (self.z <= stage)
            block = last - stage + self.z
            slot = block if stage < last else self.z * (1 - upper)
        else:
            valid = (last - self.z >= 1) & (last - self.z <= stage)
            block = stage - last + self.z
            slot = block if stage < last else self.z + (last - self.z) * (1 - upper)
        sem = 2 * stage + side
        here = self.r.zrecv[i].at[slot]

        def take():
            remote(here, here, self.r.rs.at[i, sem], self.r.rr.at[i, sem], af=self.af).wait_recv()
            use(block, slot)

        pl.when(valid)(take)

    def reduce_start(self, i):
        self.swap_copy(i).start()

    def reduce_mid(self, i):
        part, swapped, last = self.r.part[i % 4], self.r.swapped[i % 4], self.zs - 1
        self.swap_copy(i).wait_recv()

        def add(t, carry):
            part[self.c, t] = (part[self.c, t].astype(F32) + swapped[t].astype(F32)).astype(BF16)
            return carry

        lax.fori_loop(0, self.zs, add, 0)
        for side, end in ((0, 0), (1, last)):
            @pl.when(self.z == end)
            def _(side=side):
                for stage in range(1, last + 1):
                    self.flow(i, stage, side)[1]().start()

    def reduce_hop(self, i, half):
        part, hops = self.r.part[i % 4], self.zs - 2

        def add(block, slot):
            part[self.c, block] = (
                part[self.c, block].astype(F32) + self.r.zrecv[i][slot].astype(F32)
            ).astype(BF16)

        for stage in range((half - 1) * hops // 2 + 1, half * hops // 2 + 1):
            for side in (0, 1):
                self.taken(i, stage, side, add)
            for side, end in ((0, 0), (1, self.zs - 1)):
                valid, copy = self.flow(i, stage + 1, side)
                pl.when(valid & (self.z != end))(lambda copy=copy: copy().start())

    def reduce_end(self, i):
        out, last = self.r.sums[i], self.zs - 1
        out[...] = self.r.part[i % 4][self.c, self.z].astype(F32)

        def add(block, slot):
            out[...] += self.r.zrecv[i][slot].astype(F32)

        for side in (0, 1):
            self.taken(i, last, side, add)
        self.swap_copy(i).wait_send()
        for stage in range(1, last + 1):
            for side in (0, 1):
                valid, copy = self.flow(i, stage, side)
                pl.when(valid)(lambda copy=copy: copy().wait_send())

    def products(self, i, pairs):
        part, count = self.r.part[i % 4], self.count
        turn = i % 4 >= 2 and self.flip
        for group in [[pair] for pair in pairs] if turn else [pairs]:
            if turn:
                self.r.turned[...] = group[0][2][...].T

            def chip(z, carry, group=group):
                here = pl.ds(pl.multiple_of(z * 2 * count, 2 * count), 2 * count)
                for j, left, right in group:
                    if turn:
                        product = mm(self.r.turned[...], left[:, here]).astype(BF16)
                        part[0, z, j] = product[:, :count]
                        part[1, z, j] = product[:, count:]
                    else:
                        product = mm_tn(left[:, here], right[...]).astype(BF16)
                        part[0, z, j] = product[:count]
                        part[1, z, j] = product[count:]
                return carry

            lax.fori_loop(0, self.zs, chip, 0)


    def tables(self):
        r = self.r
        count = r.lengths.shape[1]
        places = lax.broadcasted_iota(jnp.int32, (self.bucket, 1), 0)
        beginning = jnp.zeros((self.bucket, 1), jnp.int32)
        end = 0
        for s in range(count):
            start, end = end, end + r.lengths[0, s]
            beginning = jnp.where((places >= start) & (places < end), start, beginning)
        angles = (places - beginning).astype(F32) * r.wave[0:1]
        r.cos[...] = jnp.cos(angles)
        r.sin[...] = jnp.sin(angles) * r.wave[1:2]

    def turning(self, where):
        copies = self.width // 128
        return (
            jnp.concatenate([self.r.cos[where]] * copies, axis=1),
            jnp.concatenate([self.r.sin[where]] * copies, axis=1),
        )

    def allowed(self, i):
        span = (i + 1) * self.rows
        places_q = i * self.rows + lax.broadcasted_iota(jnp.int32, (self.rows, 1), 0)
        places_k = lax.broadcasted_iota(jnp.int32, (1, span), 1)
        qdoc = jnp.zeros((self.rows, 1), jnp.int32)
        kdoc = jnp.zeros((1, span), jnp.int32)
        end = 0
        for s in range(self.r.lengths.shape[1]):
            end = end + self.r.lengths[0, s]
            qdoc = qdoc + (places_q >= end).astype(jnp.int32)
            kdoc = kdoc + (places_k >= end).astype(jnp.int32)
        qdoc = jnp.where(places_q >= end, -1, qdoc)
        return ((qdoc == kdoc) & (places_k <= places_q)) | (places_k == places_q)

    def matrix(self, i, j):
        return self.r.w[i][:, j].reshape(self.depth, self.r.w[i].shape[-1])

    def turned(self, i, j):
        return jnp.concatenate([self.r.w[i][owner, j] for owner in range(self.g)], axis=1)

    def into_hidden(self, source, i, j):
        return mm_nt(source, self.turned(i, j)) if self.flip else mm(source, self.matrix(i, j))

    def out_of_hidden(self, source, i, j):
        return mm(source, self.turned(i, j)) if self.flip else mm_nt(source, self.matrix(i, j))


    def project(self, layer, block):
        r = self.r
        where = rows_of(block, self.rows)
        source = r.ng[2 * layer][where]
        cosine, sine = self.turning(where)
        raw = mm(source, self.matrix(4 * layer, 0))
        r.q[layer][where] = (raw * cosine + swap_halves(raw) * sine).astype(BF16)
        raw = mm(source, self.matrix(4 * layer, 1))
        r.k[layer][where] = (raw * cosine + swap_halves(raw) * sine).astype(BF16)
        raw = mm(source, self.matrix(4 * layer, 2))
        if layer == 0:
            r.first[where] = raw
            r.v[layer][where] = raw.astype(BF16)
        else:
            r.v[layer][where] = (0.5 * raw + 0.5 * r.first[where]).astype(BF16)

    def attend(self, layer, slot):
        r, rows = self.r, self.rows
        masks, masks32 = head_masks(self.width, BF16), head_masks(self.width, F32)
        for i in range(self.n):
            span = (i + 1) * rows
            here = slice(i * rows, span)
            scores = mm_nt(stack_heads(r.q[layer][here], masks), r.k[layer][:span])
            probs = [p.astype(BF16) for p in softmax_parts(scores, self.allowed(i), self.heads, rows)]
            mixed = mm(jnp.concatenate(probs, axis=0), r.v[layer][:span])
            block = unstack_heads(mixed, masks32, rows).astype(BF16)
            r.att[layer][here] = block
            self.ship(mm_nt(block, self.matrix(4 * layer + 1, 0)), slot, i)

    def attend_back(self, layer, slot):
        r, rows = self.r, self.rows
        masks, masks32 = head_masks(self.width, BF16), head_masks(self.width, F32)
        scale = HD ** -0.5
        for i in reversed(range(self.n)):
            span = (i + 1) * rows
            here = slice(i * rows, span)
            keys, vals = r.k[layer][:span], r.v[layer][:span]
            qs = stack_heads(r.q[layer][here], masks)
            gas = stack_heads(r.gat[here], masks)
            probs = softmax_parts(mm_nt(qs, keys), self.allowed(i), self.heads, rows)
            gprobs = mm_nt(gas, vals)
            raws = []
            for h in range(self.heads):
                p, gp = probs[h], gprobs[h * rows:(h + 1) * rows]
                inner = jnp.sum(p * gp, axis=-1, keepdims=True)
                raws.append((p * (gp - inner) * scale).astype(BF16))
            raw = jnp.concatenate(raws, axis=0)
            low = jnp.concatenate([p.astype(BF16) for p in probs], axis=0)
            if i == self.n - 1:
                r.gva[...] = mm_tn(low, gas)
                r.gka[...] = mm_tn(raw, qs)
            else:
                r.gva[:span] += mm_tn(low, gas)
                r.gka[:span] += mm_tn(raw, qs)
            cosine, sine = self.turning(here)
            gqr = unstack_heads(mm(raw, keys), masks32, rows)
            gqr = (gqr * cosine - swap_halves(gqr) * sine).astype(BF16)
            gkr = r.gka[here]
            gkr = (gkr * cosine - swap_halves(gkr) * sine).astype(BF16)
            if layer == 1:
                half = 0.5 * r.gva[here]
                r.carry[here] = half
                gvr = half.astype(BF16)
            else:
                gvr = (r.gva[here] + r.carry[here]).astype(BF16)
            r.gq[here], r.gk[here], r.gv[here] = gqr, gkr, gvr
            part = (
                mm_nt(gqr, self.matrix(4 * layer, 0))
                + mm_nt(gkr, self.matrix(4 * layer, 1))
                + mm_nt(gvr, self.matrix(4 * layer, 2))
            )
            self.ship(part, slot, i)

    def gathered(self, ref, wheres):
        blocks = [ref[where] for where in wheres]
        return blocks[0] if len(blocks) == 1 else jnp.concatenate(blocks, axis=0)

    def scattered(self, ref, wheres, value):
        count = value.shape[0] // len(wheres)
        for j, where in enumerate(wheres):
            ref[where] = value[j * count:(j + 1) * count]

    def feed(self, slot, buffer, agslot, ready):
        r = self.r

        def first(wheres):
            source = self.gathered(buffer, wheres)
            g, u = self.into_hidden(source, 2, 0), self.into_hidden(source, 2, 1)
            self.scattered(r.gate, wheres, g)
            self.scattered(r.up, wheres, u)
            return g, u

        def second(g, u):
            return self.out_of_hidden((g * jax.nn.sigmoid(g) * u).astype(BF16), 3, 0)

        mine = rows_of(self.ha, self.rows)
        first([mine])
        for index, (c, ks) in enumerate(self.order):
            self.arrived(buffer, agslot, [(c, ks)])
            g, u = first([self.chunk_of(other(self.ha, k), c) for k in ks])
            if index == 0:
                ready()
            self.send_parts(slot, c, ks, second(g, u))
            if index == 0:
                r.own[...] = second(r.gate[mine], r.up[mine])

    def feed_turn(self, slot, buffer, agslot):
        r = self.r

        def branch(wheres):
            source = self.gathered(buffer, wheres)
            g, u = self.into_hidden(source, 6, 0), self.into_hidden(source, 6, 1)
            return self.feed_back(1, wheres, g, u)

        def output(wheres, h):
            self.scattered(r.ypart, wheres, self.out_of_hidden(h, 7, 0).astype(BF16))

        mine = [rows_of(self.ha, self.rows)]
        r.own[...], h = branch(mine)
        output(mine, h)
        for c, ks in self.order:
            self.arrived(buffer, agslot, [(c, ks)])
            wheres = [self.chunk_of(other(self.ha, k), c) for k in ks]
            part, h = branch(wheres)
            self.send_parts(slot, c, ks, part)
            output(wheres, h)

    def feed_return(self, slot, buffer, agslot):
        r = self.r

        def branch(wheres):
            return self.feed_back(0, wheres, self.gathered(r.gate, wheres), self.gathered(r.up, wheres))[0]

        r.own[...] = branch([rows_of(self.ha, self.rows)])
        for c, ks in self.order:
            self.arrived(buffer, agslot, [(c, ks)])
            self.send_parts(slot, c, ks, branch([self.chunk_of(other(self.ha, k), c) for k in ks]))

    def feed_back(self, layer, wheres, g, u):
        r = self.r
        s = jax.nn.sigmoid(g)
        h = (g * s * u).astype(BF16)
        gh = self.into_hidden(self.gathered(r.gg[0], wheres), 4 * layer + 3, 0)
        a = (gh * u * s * (1.0 + g * (1.0 - s))).astype(BF16)
        b = (gh * g * s).astype(BF16)
        for j, value in enumerate((a, b, h)):
            self.scattered(r.units[j], wheres, value)
        return self.out_of_hidden(a, 4 * layer + 2, 0) + self.out_of_hidden(b, 4 * layer + 2, 1), h

    def down_grads(self, layer):
        self.products(4 * layer + 3, [(0, self.r.gg[0], self.r.units[2])])
        self.reduce_start(4 * layer + 3)

    def gate_grads(self, layer):
        normed = self.r.ng[2 * layer + 1]
        self.products(4 * layer + 2, [(0, normed, self.r.units[0]), (1, normed, self.r.units[1])])
        self.reduce_start(4 * layer + 2)

    def output_grads(self, layer):
        self.products(4 * layer + 1, [(0, self.r.gg[1], self.r.att[layer])])
        self.reduce_start(4 * layer + 1)

    def head_grads(self, layer):
        r = self.r
        normed = r.ng[2 * layer]
        self.products(4 * layer, [(0, normed, r.gq), (1, normed, r.gk), (2, normed, r.gv)])
        self.reduce_start(4 * layer)


    def gain_phase(self, slot, axis, me, count, place):
        buffer = self.r.gbuf[slot]
        for t in range(count):
            copy = remote(
                buffer.at[me], buffer.at[me], self.r.gns.at[slot, t], self.r.gnr.at[slot, me], **{axis: place(t)}
            )
            pl.when(me != t)(copy.start)

    def gain_sum(self, slot, axis, me, count, place):
        buffer = self.r.gbuf[slot]
        for t in range(count):
            copy = remote(
                buffer.at[t], buffer.at[t], self.r.gns.at[slot, t], self.r.gnr.at[slot, t], **{axis: place(t)}
            )
            pl.when(me != t)(copy.wait)
        total = buffer[0]
        for t in range(1, count):
            total = total + buffer[t]
        return total

    def run(self):
        r, n = self.r, self.n
        barrier = pltpu.get_barrier_semaphore()
        for k in range(1, n):
            pl.semaphore_signal(barrier, inc=1, device_id={"ha": other(self.ha, k)}, device_id_type=MESH)
        pl.semaphore_signal(barrier, inc=1, device_id={"af": self.sibling}, device_id_type=MESH)
        for d in range(1, self.zs):
            t = lax.rem(self.z + d, self.zs)
            pl.semaphore_signal(barrier, inc=1, device_id={"af": t * 2 + self.c}, device_id_type=MESH)
        for i in range(8):
            for j in range(r.w[i].shape[1]):
                self.local_copy(i, j).start()
        mine = rows_of(self.ha, self.rows)
        x = r.x[...].astype(F32)
        r.ng[0][mine] = normalize(x, r.gains[0][...]).astype(BF16)
        r.gg[0][mine] = r.cot[...]
        pl.semaphore_wait(barrier, n - 1 + 1 + self.zs - 1)

        self.gather_start(0)
        self.gather_start(1)
        self.spread_all(r.ng[0], 0)
        self.tables()
        self.gather_hop(0, 1)
        self.gather_start(2)
        self.arrived(r.ng[0], 0, self.near)
        self.gather_hop(1, 1)
        self.gather_hop(0, 2)
        self.arrived(r.ng[0], 0, self.far)
        self.gather_hop(1, 2)
        self.gather_hop(0, 3)
        self.gather_end(0)
        for k in range(n):
            self.project(0, other(self.ha, k))
        self.gather_hop(1, 3)
        self.gather_end(1)
        self.gather_hop(2, 1)
        self.gather_start(3)
        self.attend(0, 0)
        self.gather_hop(2, 2)

        for c in range(self.chunks):
            here = self.chunk(c)
            value = x[here] + self.collect(0, c)
            r.middle[0][here] = value
            r.ng[1][self.chunk_of(self.ha, c)] = normalize(value, r.gains[1][...]).astype(BF16)
            self.spread(r.ng[1], 2, c)
        self.parts_done(0)
        self.gather_hop(3, 1)
        self.gather_start(4)
        self.gather_start(5)
        self.gather_hop(2, 3)
        self.gather_end(2)
        self.gather_hop(3, 2)

        def ready():
            self.spread_all(r.gg[0], 1)
            self.gather_hop(3, 3)
            self.gather_start(6)
            self.gather_end(3)

        self.feed(1, r.ng[1], 2, ready)
        for third in (1, 2):
            self.gather_hop(4, third)
            self.gather_hop(5, third)

        for c in range(self.chunks):
            here = self.chunk(c)
            value = r.middle[0][here] + self.collect(1, c)
            r.between[here] = value
            r.ng[2][self.chunk_of(self.ha, c)] = normalize(value, r.gains[2][...]).astype(BF16)
            self.spread(r.ng[2], 3, c)
        self.parts_done(1)
        self.gather_hop(4, 3)
        self.gather_hop(5, 3)
        self.gather_start(7)
        self.gather_end(4)
        self.each_block(r.ng[2], 3, functools.partial(self.project, 1))
        self.gather_hop(6, 1)
        self.arrived(r.gg[0], 1, self.near)
        self.gather_end(5)
        self.attend(1, 2)
        self.gather_hop(6, 2)
        self.gather_hop(7, 1)
        self.gather_hop(6, 3)

        for c in range(self.chunks):
            here = self.chunk(c)
            value = r.between[here] + self.collect(2, c)
            r.middle[1][here] = value
            r.ng[3][self.chunk_of(self.ha, c)] = normalize(value, r.gains[3][...]).astype(BF16)
            self.spread(r.ng[3], 4, c)
        self.parts_done(2)
        self.gather_hop(7, 2)
        self.gather_end(6)
        self.arrived(r.gg[0], 1, self.far)
        self.gather_hop(7, 3)
        self.gather_end(7)
        self.feed_turn(3, r.ng[3], 4)
        self.down_grads(1)
        self.gate_grads(1)
        self.reduce_mid(7)
        self.spread_done(r.gg[0], 1)

        gain = 0.0
        for c in range(self.chunks):
            here = self.chunk(c)
            back, share = norm_back(r.middle[1][here], r.gains[3][...], self.collect(3, c))
            gain = gain + share
            value = r.cot[here].astype(F32) + back
            r.gmid[here] = value
            r.gg[1][self.chunk_of(self.ha, c)] = value.astype(BF16)
            self.spread(r.gg[1], 5, c)
        r.gsum[3:4] = gain
        self.parts_done(3)
        self.reduce_mid(6)
        self.reduce_hop(7, 1)
        self.pull(1, 5)
        for k in range(3, n):
            self.output_copy(k).start()
        self.reduce_hop(7, 2)
        self.output_grads(1)
        self.reduce_hop(6, 1)
        self.attend_back(1, 4)
        self.reduce_end(7)
        self.reduce_mid(5)
        self.reduce_hop(6, 2)
        self.head_grads(1)
        self.reduce_hop(5, 1)
        self.reduce_mid(4)
        self.spread_done(r.gg[1], 5)

        gain = 0.0
        for c in range(self.chunks):
            here = self.chunk(c)
            back, share = norm_back(r.between[here], r.gains[2][...], self.collect(4, c))
            gain = gain + share
            value = r.gmid[here] + back
            r.between[here] = value
            r.gg[0][self.chunk_of(self.ha, c)] = value.astype(BF16)
            self.spread(r.gg[0], 6, c)
        r.gsum[2:3] = gain
        self.parts_done(4)
        self.reduce_hop(5, 2)
        self.reduce_end(6)
        self.reduce_hop(4, 1)
        self.feed_return(5, r.gg[0], 6)
        self.down_grads(0)
        self.reduce_end(5)
        self.reduce_hop(4, 2)
        self.gate_grads(0)
        self.reduce_mid(3)
        self.reduce_end(4)

        gain = 0.0
        for c in range(self.chunks):
            here = self.chunk(c)
            back, share = norm_back(r.middle[0][here], r.gains[1][...], self.collect(5, c))
            gain = gain + share
            value = r.between[here] + back
            r.gmid[here] = value
            r.gg[1][self.chunk_of(self.ha, c)] = value.astype(BF16)
            self.spread(r.gg[1], 7, c)
        r.gsum[1:2] = gain
        self.parts_done(5)
        self.reduce_mid(2)
        self.reduce_hop(3, 1)
        self.pull(0, 7)
        for k in (1, 2):
            self.output_copy(k).start()
        self.reduce_hop(3, 2)
        self.output_grads(0)
        self.reduce_hop(2, 1)
        self.attend_back(0, 6)
        self.reduce_mid(1)
        self.reduce_hop(2, 2)
        self.head_grads(0)
        self.reduce_end(3)
        self.reduce_hop(1, 1)
        self.reduce_mid(0)
        gain = 0.0
        for c in range(self.chunks):
            here = self.chunk(c)
            back, share = norm_back(x[here], r.gains[0][...], self.collect(6, c))
            gain = gain + share
            r.gx[here] = r.gmid[here] + back
        r.gsum[0:1] = gain
        self.parts_done(6)

        r.gbuf[0][self.ha] = r.gsum[...]
        self.gain_phase(0, "ha", self.ha, n, lambda t: t)
        out = r.middle[1][...] + r.ypart[mine].astype(F32)
        for k in range(1, n):
            self.output_copy(k).wait_recv()
            out = out + r.yrecv[k].astype(F32)
        r.out[...] = out.astype(BF16)
        self.reduce_hop(1, 2)
        self.reduce_hop(0, 1)
        r.gbuf[1][self.c] = self.gain_sum(0, "ha", self.ha, n, lambda t: t)
        self.gain_phase(1, "af", self.c, 2, lambda t: self.z * 2 + t)
        self.reduce_end(2)
        r.gbuf[2][self.z] = self.gain_sum(1, "af", self.c, 2, lambda t: self.z * 2 + t)
        self.gain_phase(2, "af", self.z, self.zs, lambda t: t * 2 + self.c)
        self.reduce_hop(0, 2)
        self.reduce_end(1)
        total = self.gain_sum(2, "af", self.z, self.zs, lambda t: t * 2 + self.c)
        for i in range(4):
            r.gainsum[i] = total[i:i + 1]
        self.reduce_end(0)
        for slot, buffer in ((0, r.ng[0]), (2, r.ng[1]), (3, r.ng[2]), (4, r.ng[3]), (6, r.gg[0]), (7, r.gg[1])):
            self.spread_done(buffer, slot)
        for k in range(1, n):
            self.output_copy(k).wait_send()
        for i in range(8):
            self.gather_drain(i)

    def pull(self, layer, slot):
        r = self.r

        def block(owner):
            where = rows_of(owner, self.rows)
            r.gat[where] = mm(r.gg[1][where], self.matrix(4 * layer + 1, 0)).astype(BF16)

        self.each_block(r.gg[1], slot, block)


def step_kernel(n, g, names, *refs):
    found = {}
    for (name, index), ref in zip(names, refs):
        if index is None:
            found[name] = ref
        else:
            found.setdefault(name, {})[index] = ref
    Step(n, g, types.SimpleNamespace(**found)).run()


def finish_kernel(*refs):
    sums, gains, out, gx = refs[:8], refs[8], refs[9], refs[10]
    results, held, sem = refs[11:31], refs[31:-1], refs[-1]
    pairs = [(out, 0), (gx, 1)]
    for layer in range(2):
        first = 2 + 9 * layer
        pairs += [(gains.at[2 * layer], first), (gains.at[2 * layer + 1], first + 5)]
        pairs += [(sums[4 * layer].at[j], first + 1 + j) for j in range(3)]
        pairs.append((sums[4 * layer + 1].at[0], first + 4))
        pairs += [(sums[4 * layer + 2].at[j], first + 6 + j) for j in range(2)]
        pairs.append((sums[4 * layer + 3].at[0], first + 8))
    into = [pltpu.make_async_copy(source, held[k], sem.at[0, k]) for source, k in pairs]
    onward = [pltpu.make_async_copy(held[k], results[k], sem.at[1, k]) for _, k in pairs]
    for copy in into:
        copy.start()
    for first, second in zip(into, onward):
        first.wait()
        second.start()
    for copy in onward:
        copy.wait()


def per_device(
    block_input, lengths, cotangent,
    attngain_early, query_early, keys_early, values_early, output_early,
    ffngain_early, gate_early, upward_early, down_early,
    attngain_later, query_later, keys_later, values_later, output_later,
    ffngain_later, gate_later, upward_later, down_later,
):
    n, g = lax.axis_size("ha"), lax.axis_size("af")
    zs = g // 2
    chunks = CHUNKS if n == 4 else 1
    rows, depth = block_input.shape
    bucket = rows * n
    wrows, width = query_early.shape
    hidden = gate_early.shape[1]
    lane = np.arange(128)
    halfway = HD // 2
    frequency = np.float32(rope_base) ** (-(lane % halfway).astype(np.float32) / np.float32(halfway))
    wave = jnp.asarray(np.stack([frequency, np.where(lane % HD < halfway, -1.0, 1.0)]).astype(np.float32))
    flip = wrows % 128 == 0
    if flip:
        gate_early, upward_early, down_early = gate_early.T, upward_early.T, down_early.T
        gate_later, upward_later, down_later = gate_later.T, upward_later.T, down_later.T
    groups = [
        (query_early, keys_early, values_early), (output_early,), (gate_early, upward_early), (down_early,),
        (query_later, keys_later, values_later), (output_later,), (gate_later, upward_later), (down_later,),
    ]
    gains = [v[None, :] for v in (attngain_early, ffngain_early, attngain_later, ffngain_later)]

    names, args, in_specs = [], [], []

    def take(name, index, value, spec=VMEM):
        names.append((name, index))
        args.append(value)
        in_specs.append(spec)

    take("x", None, block_input)
    take("cot", None, cotangent)
    take("lengths", None, lengths, pl.BlockSpec(memory_space=pltpu.SMEM))
    take("wave", None, wave)
    for i, v in enumerate(gains):
        take("gains", i, v)
    for i, group in enumerate(groups):
        for j, v in enumerate(group):
            take("whbm", (i, j), v, ANY)

    outs = []

    def give(name, index, shape, kind):
        names.append((name, index))
        outs.append(jax.ShapeDtypeStruct(shape, kind))

    blocks = [(len(group), *group[0].shape) for group in groups]
    for i, shape in enumerate(blocks):
        give("sums", i, shape, F32)
    give("gainsum", None, (4, 1, depth), F32)
    give("out", None, (rows, depth), BF16)
    give("gx", None, (rows, depth), F32)

    scratch = []

    def hold(name, index, shape, kind):
        names.append((name, index))
        scratch.append(pltpu.VMEM(shape, kind))

    for i, group in enumerate(groups):
        hold("w", i, (g, len(group), *group[0].shape), BF16)
    for i in range(8):
        hold("zrecv", i, (zs, *blocks[i]), BF16)
    for i in range(4):
        hold("ng", i, (bucket, depth), BF16)
        hold("part", i, (2, zs, *blocks[i]), BF16)
        hold("swapped", i, (zs, *blocks[i]), BF16)
    for i in range(2):
        hold("gg", i, (bucket, depth), BF16)
        for name in ("q", "k", "v", "att"):
            hold(name, i, (bucket, width), BF16)
        hold("middle", i, (rows, depth), F32)
    for name in ("cos", "sin"):
        hold(name, None, (bucket, 128), F32)
    for name in ("first", "carry", "gva", "gka"):
        hold(name, None, (bucket, width), F32)
    for name in ("gat", "gq", "gk", "gv"):
        hold(name, None, (bucket, width), BF16)
    for name in ("gate", "up"):
        hold(name, None, (bucket, hidden), F32)
    for i in range(3):
        hold("units", i, (bucket, hidden), BF16)
    if flip:
        hold("turned", None, (hidden, bucket), BF16)
    for name in ("own", "between", "gmid"):
        hold(name, None, (rows, depth), F32)
    for name in ("sbuf", "rbuf", "yrecv"):
        hold(name, None, (n, rows, depth), BF16)
    hold("ypart", None, (bucket, depth), BF16)
    hold("gsum", None, (4, depth), F32)
    for i, count in enumerate((n, 2, zs)):
        hold("gbuf", i, (count, 4, depth), F32)
    for name, shape in (
        ("ags", (8, n, chunks)), ("agr", (8, n, chunks)), ("pss", (8, n, chunks)), ("psr", (8, n, chunks)), ("lsem", (8, 3)),
        ("gs", (8, 2, 2 * zs)), ("gr", (8, 2, zs)), ("rs", (8, 2 * zs)), ("rr", (8, 2 * zs)),
        ("gns", (3, max(n, zs))), ("gnr", (3, max(n, zs))),
    ):
        names.append((name, None))
        scratch.append(pltpu.SemaphoreType.DMA(shape))

    results = pl.pallas_call(
        functools.partial(step_kernel, n, g, names),
        out_shape=outs, in_specs=in_specs, out_specs=[VMEM] * len(outs), scratch_shapes=scratch,
        compiler_params=pltpu.CompilerParams(
            collective_id=0, has_side_effects=True, vmem_limit_bytes=63 * 1024 * 1024
        ),
        cost_estimate=pl.CostEstimate(flops=2 * 10**10, bytes_accessed=10**7, transcendentals=0),
        name="step",
    )(*args)

    shape = jax.ShapeDtypeStruct
    layer = (
        [shape((1, depth), F32)] + [shape((wrows, width), F32)] * 4
        + [shape((1, depth), F32)] + [shape(down_early.shape, F32)] * 3
    )
    final_shapes = [shape((rows, depth), BF16), shape((rows, depth), F32), *layer, *layer]
    finals = pl.pallas_call(
        finish_kernel,
        out_shape=final_shapes, in_specs=[ANY] * 11, out_specs=[ANY] * 20,
        scratch_shapes=[*(pltpu.VMEM(v.shape, v.dtype) for v in final_shapes), pltpu.SemaphoreType.DMA((2, 20))],
        compiler_params=pltpu.CompilerParams(vmem_limit_bytes=62 * 1024 * 1024), name="finish",
    )(*results)
    finals = [v[0] if v.shape[0] == 1 else v for v in finals]
    if flip:
        finals = [v.T if v.shape == down_early.shape else v for v in finals]
    return tuple(finals)


def solution(mesh):
    tokens = P(("af", "ha"), None)
    matrix = P("af", "ha")
    layer = (P(), matrix, matrix, matrix, matrix, P(), matrix, matrix, matrix)
    return jax.shard_map(
        per_device, mesh=mesh,
        in_specs=(tokens, P("af", None), tokens, *layer, *layer),
        out_specs=(tokens, tokens, *layer, *layer),
        check_vma=False,
    )
```
